512 devices in a mesh: gx: 64 (over z, y), gz: 8 (over x, core).
Axes of the slice: x: 4, y: 8, z: 8, core: 2. Of those that a mesh axis runs over, the one named last changes fastest.
Arguments:
- flow: float32 [4, 64, 2048, 128], P(None, 'gz', 'gx'), may hold values from -6 to 6
- fluid: float32 [64, 2048, 128], P('gz', 'gx'), may hold values from 0.2 to 5
- density: float32 [64, 2048, 128], P('gz', 'gx'), may hold values from 0.35 to 0.92
- thickness: float32 [2048, 128], P('gx'), may hold values from 0.5 to 4
- bed: float32 [2048, 128], P('gx'), may hold values from -6 to 6
- smb: float32 [2048, 128], P('gx'), may hold values from -3 to 3
- mask: int32 [2048, 128], P('gx'), may hold values from 0 to 2
Outputs:
- flow_out: float32 [4, 64, 2048, 128], P(None, 'gz', 'gx')
- new_thickness: float32 [2048, 128], P('gx')
- overburden: float32 [64, 2048, 128], P('gz', 'gx')
The draws below stay inside these ranges and needn't reach their ends.
Inputs may be any that keep to these rules, and one draw needn't show every extreme that they name: `mask`: 0 marks an ice-free column, 1 grounded ice, 2 floating ice.
All inputs are finite; a program needn't handle non-finite values.
Results may differ from the reference program's by a relative error of at most 0.00002.
Values sent between devices are 32-bit elements; how exact they have to be, the bound alone decides.
No kernel may reach another device: no remote copies, remote signals or barrier semaphores. Data moves between devices by JAX's collectives and lax.ppermute only.
A program may use at most 64 MiB of HBM per device.

```python
import math
import jax
import jax.numpy as jnp

NY = 128
ITERS = 2
NZ = 64
NX = 2048


def set_ends(values, own_key, low, largest):
    place = [jax.random.randint(jax.random.fold_in(own_key, axis), (), 0, length) for axis, length in enumerate(values.shape)]
    widest = values.shape.index(max(values.shape))
    next_to = place[:widest] + [(place[widest] + 1) % values.shape[widest]] + place[widest + 1:]
    return values.at[tuple(place)].set(low).at[tuple(next_to)].set(largest)


def level_of(key, shape, pieces, smallest, top_value):
    def one(axis_at, parts):
        heights = jax.random.uniform(jax.random.fold_in(jax.random.fold_in(key, 6), axis_at), (parts,), jnp.float32, smallest / len(pieces), top_value / len(pieces))
        return jnp.repeat(jnp.exp(heights), shape[axis_at] // parts).reshape((-1,) + (1,) * (len(shape) - axis_at - 1))

    loudness = one(*pieces[0])
    for cut in pieces[1:]:
        loudness = loudness * one(*cut)
    return loudness


def gaussian(key, dims, deviation, most, pieces=(), held_as=jnp.bfloat16):
    loudness = level_of(key, dims, pieces, -0.22, 0.18) if pieces else 1.0
    entries = jax.random.normal(key, dims, jnp.float32) * deviation * loudness
    return jnp.minimum(jnp.maximum(entries, -most), most).astype(held_as)


def setup_inputs(seed: int = 0) -> dict:
    seeds = jax.random.split(jax.random.key(seed), 8)
    flow = gaussian(seeds[0], (4, NZ, NX, NY), 1.0, 6.0, ((1, 8), (2, 64)), jnp.float32)
    fluid = jnp.clip(jnp.exp(math.log(5.0) - 3.218876 * jax.random.uniform(seeds[1], (NZ, NX, NY), jnp.float32) ** level_of(seeds[1], (NZ, NX, NY), ((0, 8), (1, 64)), -0.2, 0.2)), 0.2, 5.0)
    density = jnp.clip(0.35 + 0.570000023 * jax.random.uniform(seeds[2], (NZ, NX, NY), jnp.float32) ** level_of(seeds[2], (NZ, NX, NY), ((0, 8), (1, 64)), -0.2, 0.2), 0.35, 0.92)
    thickness = jnp.clip(jnp.exp(math.log(4.0) - 2.0794415 * jax.random.uniform(seeds[3], (NX, NY), jnp.float32) ** level_of(seeds[3], (NX, NY), ((0, 64),), -0.2, 0.2)), 0.5, 4.0)
    bed = gaussian(seeds[4], (NX, NY), 1.0, 6.0, ((0, 64),), jnp.float32)
    smb = gaussian(seeds[5], (NX, NY), 0.5, 3.0, ((0, 64),), jnp.float32)
    mask = set_ends(jax.random.randint(seeds[6], (NX, NY), 0, 3), jax.random.fold_in(seeds[6], 1), 0, 2).astype(jnp.int32)
    return {"flow": flow, "fluid": fluid, "density": density, "thickness": thickness, "bed": bed, "smb": smb, "mask": mask}


REGULAR = 0.01
FRICTION = 2.0
VELOCITY_STEP = 0.2
PRESSURE_STEP = 0.2
TIME_STEP = 0.5


def central(field, direction):
    lead = field.ndim - 3
    upper = []
    lower = []
    for number in range(field.ndim):
        extent = field.shape[number]
        if number < lead:
            upper.append(slice(None))
            lower.append(slice(None))
        elif number == lead + direction:
            upper.append(slice(2, extent))
            lower.append(slice(0, extent - 2))
        else:
            upper.append(slice(1, extent - 1))
            lower.append(slice(1, extent - 1))
    return 0.5 * (field[tuple(upper)] - field[tuple(lower)])


def stresses(padded, fluidity):
    speed_x = padded[0]
    speed_y = padded[1]
    speed_z = padded[2]
    strain_xx = central(speed_x, 1)
    strain_yy = central(speed_y, 2)
    strain_zz = central(speed_z, 0)
    strain_xy = 0.5 * (central(speed_x, 2) + central(speed_y, 1))
    strain_xz = 0.5 * (central(speed_x, 0) + central(speed_z, 1))
    strain_yz = 0.5 * (central(speed_y, 0) + central(speed_z, 2))
    second = 0.5 * (strain_xx * strain_xx + strain_yy * strain_yy + strain_zz * strain_zz)
    second = second + strain_xy * strain_xy + strain_xz * strain_xz + strain_yz * strain_yz
    viscous = 0.5 * jnp.power(fluidity, -1.0 / 3.0) * jnp.power(second + REGULAR, -1.0 / 3.0)
    stress = 2.0 * viscous[None] * jnp.stack([strain_xx, strain_yy, strain_zz, strain_xy, strain_xz, strain_yz])
    return stress, viscous, strain_xx + strain_yy + strain_zz


def momentum(stress_padded, pressure_padded):
    force_x = central(stress_padded[0], 1) + central(stress_padded[3], 2) + central(stress_padded[4], 0) - central(pressure_padded, 1)
    force_y = central(stress_padded[3], 1) + central(stress_padded[1], 2) + central(stress_padded[5], 0) - central(pressure_padded, 2)
    force_z = central(stress_padded[4], 1) + central(stress_padded[5], 2) + central(stress_padded[2], 0) - central(pressure_padded, 0)
    return force_x, force_y, force_z


def advance(state, forces, viscous, dilation, slope_x, slope_y, ice, grounded, bottom):
    force_x = forces[0] - slope_x[None] - FRICTION * grounded[None] * bottom * state[0]
    force_y = forces[1] - slope_y[None] - FRICTION * grounded[None] * bottom * state[1]
    force_z = forces[2]
    moved = jnp.stack([
        state[0] + VELOCITY_STEP * force_x / viscous,
        state[1] + VELOCITY_STEP * force_y / viscous,
        state[2] + VELOCITY_STEP * force_z / viscous,
        state[3] - PRESSURE_STEP * viscous * dilation,
    ])
    return moved * ice[None, None]


def plane_slopes(padded):
    slope_x = 0.5 * (padded[2:, 1:-1] - padded[:-2, 1:-1])
    slope_y = 0.5 * (padded[1:-1, 2:] - padded[1:-1, :-2])
    return slope_x, slope_y


def reference(flow, fluid, density, thickness, bed, smb, mask):
    surface = bed + thickness
    slope_x, slope_y = plane_slopes(jnp.pad(surface, 1))
    ice = (mask > 0).astype(jnp.float32)
    grounded = (mask == 1).astype(jnp.float32)
    bottom = (jnp.arange(NZ) == 0).astype(jnp.float32)[:, None, None]
    state = flow
    widths = ((0, 0), (1, 1), (1, 1), (1, 1))
    for sweep in range(ITERS):
        padded = jnp.pad(state, widths)
        stress, viscous, dilation = stresses(padded, fluid)
        forces = momentum(jnp.pad(stress, widths), padded[3])
        state = advance(state, forces, viscous, dilation, slope_x, slope_y, ice, grounded, bottom)
    fluxes = thickness[None] * jnp.sum(state[:2], axis=1) / NZ
    flux_padded = jnp.pad(fluxes, ((0, 0), (1, 1), (1, 1)))
    spread = 0.5 * (flux_padded[0, 2:, 1:-1] - flux_padded[0, :-2, 1:-1])
    spread = spread + 0.5 * (flux_padded[1, 1:-1, 2:] - flux_padded[1, 1:-1, :-2])
    new_thickness = thickness + TIME_STEP * (smb - spread)
    suffix = jnp.flip(jnp.cumsum(jnp.flip(density, 0), 0), 0) - density
    overburden = new_thickness[None] * (suffix + 0.5 * density) / NZ
    return state, new_thickness, overburden
```

```python
import jax
import jax.numpy as jnp
from jax import lax
from jax.experimental import pallas as pl
from jax.experimental.pallas import tpu as pltpu
from jax.sharding import PartitionSpec as P

REGULAR = 0.01

DEEP = 4
WIDE = 5
WINDOW = 4
MARGIN = 8
VMEM_LIMIT = 24 * 1024 * 1024


def call(kernel, outs, scratch=(), aliases=None, cost=None):
    return pl.pallas_call(
        kernel,
        out_shape=outs,
        scratch_shapes=scratch,
        input_output_aliases=aliases or {},
        compiler_params=pltpu.CompilerParams(vmem_limit_bytes=VMEM_LIMIT),
        cost_estimate=cost,
    )


def f32(*shape):
    return jax.ShapeDtypeStruct(shape, jnp.float32)


def pack_columns(flow, fluid, bed, thickness, mask, low, high):
    parts, levels, columns, _ = flow.shape
    for out, start in ((low, 0), (high, columns - WIDE)):
        edge = slice(start, start + WIDE)
        place = 0
        for part in range(parts):
            for level in range(levels):
                out[place : place + WIDE, :] = flow[part, level, edge, :]
                place += WIDE
        for level in range(levels):
            out[place : place + WIDE, :] = fluid[level, edge, :]
            place += WIDE
        height = thickness[edge, :]
        out[place : place + WIDE, :] = bed[edge, :] + height
        out[place + WIDE : place + 2 * WIDE, :] = height
        out[place + 2 * WIDE : place + 3 * WIDE, :] = mask[edge, :].astype(jnp.float32)


def pack_levels(flow, fluid, left, right, low, high):
    parts, levels, columns, _ = flow.shape
    rows = columns + 2 * WINDOW
    skip = WIDE - WINDOW
    first = lax.axis_index("gx") == 0
    last = lax.axis_index("gx") == lax.axis_size("gx") - 1
    for out, start in ((low, 0), (high, levels - DEEP)):
        place = 0
        for part in range(parts + 1):
            for number in range(DEEP):
                level = start + number
                if part >= parts - 1 and number == (DEEP - 1 if start == 0 else 0):
                    continue
                own = flow.at[part, level] if part < parts else fluid.at[level]
                at = (part * levels + level) * WIDE
                before = left[at + skip : at + WIDE, :]
                after = right[at : at + WINDOW, :]
                if part == parts:
                    before = jnp.where(first, jnp.inf, before)
                    after = jnp.where(last, jnp.inf, after)
                out[place : place + WINDOW, :] = before
                out[place + WINDOW : place + WINDOW + columns, :] = own[...]
                out[place + WINDOW + columns : place + rows, :] = after
                place += rows


def assemble(flow, fluid, bed, thickness, mask, left, right, state, planes):
    parts, levels, columns, _ = flow.shape
    rows = columns + 2 * WINDOW
    lead = MARGIN + WINDOW
    first = lax.axis_index("gx") == 0
    last = lax.axis_index("gx") == lax.axis_size("gx") - 1
    for part in range(parts + 1):
        for level in range(levels):
            at = (part * levels + level) * WIDE
            own = flow[part, level] if part < parts else fluid[level]
            before = left[at : at + WIDE, :]
            after = right[at : at + WIDE, :]
            if part == parts:
                before = jnp.where(first, jnp.inf, before)
                after = jnp.where(last, jnp.inf, after)
            state[part, DEEP + level, lead - WIDE : lead, :] = before
            state[part, DEEP + level, lead : lead + columns, :] = own
            state[part, DEEP + level, lead + columns : lead + columns + WIDE, :] = after
    at = (parts + 1) * levels * WIDE
    for number, own in enumerate((bed[...] + thickness[...], thickness[...], mask[...].astype(jnp.float32))):
        spot = at + number * WIDE
        planes[number, lead - WIDE : lead, :] = left[spot : spot + WIDE, :]
        planes[number, lead : lead + columns, :] = own
        planes[number, lead + columns : lead + columns + WIDE, :] = right[spot : spot + WIDE, :]


def along_y(field):
    lane = lax.broadcasted_iota(jnp.int32, field.shape, 1)
    end = field.shape[1] - 1
    upper = jnp.where(lane < end, pltpu.roll(field, end, 1), 0.0)
    lower = jnp.where(lane > 0, pltpu.roll(field, 1, 1), 0.0)
    return upper - lower


def evolve(state_in, planes, below, above, density, out, message, state, stress, extra, slopes, marks):
    parts, levels, columns, lanes = out.shape
    rows = columns + 2 * WINDOW
    deep = levels + 2 * DEEP
    win = slice(MARGIN, MARGIN + rows)
    ahead = slice(MARGIN + 1, MARGIN + rows + 1)
    behind = slice(MARGIN - 1, MARGIN + rows - 1)
    lowest = lax.axis_index("gz") == 0
    highest = lax.axis_index("gz") == lax.axis_size("gz") - 1

    for part in range(parts + 1):
        for level in range(levels):
            state[part, DEEP + level] = state_in[part, DEEP + level]
    for source, start, outside in ((below, 0, lowest), (above, DEEP + levels, highest)):
        place = 0
        for part in range(parts + 1):
            for number in range(DEEP):
                if part >= parts - 1 and number == (0 if start == 0 else DEEP - 1):
                    continue
                plane = source[place : place + rows, :]
                if part == parts:
                    plane = jnp.where(outside, jnp.inf, plane)
                state[part, start + number, win, :] = plane
                place += rows

    slopes[0] = 4.0 * (planes[0, ahead, :] - planes[0, behind, :])
    slopes[1] = 4.0 * along_y(planes[0, win, :])
    kind = planes[2, win, :]
    ice = jnp.where(kind > 0.5, 1.0, 0.0)
    marks[0] = jnp.where(lowest, 0.0, ice)
    marks[1] = ice
    marks[2] = jnp.where(highest, 0.0, ice)
    marks[3] = jnp.zeros_like(ice)
    marks[4] = jnp.where(lowest & (kind > 0.5) & (kind < 1.5), 16.0, 0.0)

    def strain(k, carry):
        def across(part):
            return state[part, k, ahead, :] - state[part, k, behind, :]

        def upward(part):
            return state[part, k + 1, win, :] - state[part, k - 1, win, :]

        xx = across(0)
        yy = along_y(state[1, k, win, :])
        zz = upward(2)
        xy = along_y(state[0, k, win, :]) + across(1)
        xz = upward(0) + across(2)
        yz = upward(1) + along_y(state[2, k, win, :])
        second = 2.0 * (xx * xx + yy * yy + zz * zz) + (xy * xy + xz * xz + yz * yz)
        base = state[4, k, win, :] * (second * 0.0625 + REGULAR)
        root = jnp.exp2(jnp.log2(base) * (-1.0 / 3.0))
        pressure = state[3, k, win, :]
        push = 4.0 * pressure
        twice = 2.0 * root
        stress[0, k, win, :] = twice * xx - push
        stress[1, k, win, :] = twice * yy - push
        stress[2, k, win, :] = twice * zz - push
        stress[3, k, win, :] = root * xy
        stress[4, k, win, :] = root * xz
        stress[5, k, win, :] = root * yz
        extra[0, k] = 0.05 * (base * (root * root))
        extra[1, k] = pressure - (0.05 * root) * (xx + yy + zz)
        return carry

    def forces(k):
        def across(which):
            return stress[which, k, ahead, :] - stress[which, k, behind, :]

        def upward(which):
            return stress[which, k + 1, win, :] - stress[which, k - 1, win, :]

        def sideways(which):
            return along_y(stress[which, k, win, :])

        factor = extra[0, k]
        inside = marks[(k >= DEEP).astype(jnp.int32) + (k >= DEEP + levels).astype(jnp.int32)] > 0.5
        drag = marks[3 + (k == DEEP).astype(jnp.int32)]
        u = state[0, k, win, :]
        v = state[1, k, win, :]
        w = state[2, k, win, :]
        force_x = across(0) + sideways(3) + upward(4) - slopes[0] - drag * u
        force_y = across(3) + sideways(1) + upward(5) - slopes[1] - drag * v
        force_z = across(4) + sideways(5) + upward(2)
        return (
            jnp.where(inside, u + factor * force_x, 0.0),
            jnp.where(inside, v + factor * force_y, 0.0),
            jnp.where(inside, w + factor * force_z, 0.0),
            jnp.where(inside, extra[1, k], 0.0),
        )

    def first(k, carry):
        for part, value in enumerate(forces(k)):
            state[part, k, win, :] = value
        return carry

    own = slice(WINDOW, WINDOW + columns)

    def second(k, carry):
        values = forces(k)
        for part, value in enumerate(values):
            out[part, k - DEEP] = value[own, :]
        return carry[0] + values[0], carry[1] + values[1]

    lax.fori_loop(1, deep - 1, strain, 0)
    lax.fori_loop(2, deep - 2, first, 0)
    lax.fori_loop(3, deep - 3, strain, 0)
    nothing = jnp.zeros((rows, lanes), jnp.float32)
    sum_u, sum_v = lax.fori_loop(DEEP, deep - DEEP, second, (nothing, nothing))

    half = 0.5 / (levels * lax.axis_size("gz"))
    height = planes[1, win, :]
    slopes[0] = height * sum_u
    flux_y = along_y(height * sum_v)
    flux_x = slopes[0, WINDOW + 1 : WINDOW + columns + 1, :] - slopes[0, WINDOW - 1 : WINDOW + columns - 1, :]
    spread = half * (flux_x + flux_y[own, :])
    weight = jnp.sum(density[...], axis=0)
    for target in range(message.shape[0]):
        message[target, :columns, :] = spread
        message[target, columns:, :] = weight


def finish(message, density, thickness, smb, grown, burden):
    devices = message.shape[0]
    levels, columns, _ = density.shape
    place = lax.axis_index("gz")
    spread = message[0, :columns, :]
    over = jnp.where(place < 0, message[0, columns:, :], 0.0)
    for device in range(1, devices):
        spread = spread + message[device, :columns, :]
        over = over + jnp.where(place < device, message[device, columns:, :], 0.0)
    new = thickness[...] + 0.5 * (smb[...] - spread)
    grown[...] = new
    scaled = new * (1.0 / (levels * devices))
    for level in range(levels - 1, -1, -1):
        here = density[level]
        burden[level] = scaled * (over + 0.5 * here)
        over = over + here


def shifts(count):
    up = [(i, i + 1) for i in range(count - 1)]
    return up, [(j, i) for i, j in up]


def body(flow, fluid, density, thickness, bed, smb, mask):
    parts, levels, columns, lanes = flow.shape
    rows = columns + 2 * WINDOW
    deep = levels + 2 * DEEP
    tall = rows + 2 * MARGIN
    right_way, left_way = shifts(lax.axis_size("gx"))
    up_way, down_way = shifts(lax.axis_size("gz"))

    side = f32(((parts + 1) * levels + 3) * WIDE, lanes)
    to_left, to_right = call(pack_columns, (side, side))(flow, fluid, bed, thickness, mask)
    left = lax.ppermute(to_right, "gx", right_way)
    right = lax.ppermute(to_left, "gx", left_way)

    face = f32(((parts + 1) * DEEP - 2) * rows, lanes)
    to_below, to_above = call(pack_levels, (face, face))(flow, fluid, left, right)
    below = lax.ppermute(to_above, "gz", up_way)
    above = lax.ppermute(to_below, "gz", down_way)

    wide = f32(parts + 1, deep, tall, lanes)
    state, planes = call(
        assemble,
        (wide, f32(3, tall, lanes)),
        cost=pl.CostEstimate(flops=10_000_000, bytes_accessed=4_000_000, transcendentals=0),
    )(flow, fluid, bed, thickness, mask, left, right)

    message = f32(lax.axis_size("gz"), 2 * columns, lanes)
    moved, message = call(
        evolve,
        (f32(*flow.shape), message),
        scratch=[
            pltpu.VMEM((parts + 1, deep, tall, lanes), jnp.float32),
            pltpu.VMEM((6, deep, tall, lanes), jnp.float32),
            pltpu.VMEM((2, deep, rows, lanes), jnp.float32),
            pltpu.VMEM((2, rows, lanes), jnp.float32),
            pltpu.VMEM((5, rows, lanes), jnp.float32),
        ],
    )(state, planes, below, above, density)
    message = lax.all_to_all(message, "gz", split_axis=0, concat_axis=0, tiled=True)
    grown, burden = call(finish, (f32(columns, lanes), f32(*density.shape)))(message, density, thickness, smb)
    return moved, grown, burden


def solution(mesh):
    level_split = P("gz", "gx", None)
    flat = P("gx", None)
    return jax.shard_map(
        body,
        mesh=mesh,
        in_specs=(P(None, "gz", "gx", None), level_split, level_split, flat, flat, flat, flat),
        out_specs=(P(None, "gz", "gx", None), flat, level_split),
        check_vma=False,
    )
```

```python
import functools

import jax
import jax.numpy as jnp
from jax import lax
from jax.experimental import pallas as pl
from jax.experimental.pallas import tpu as pltpu
from jax.sharding import PartitionSpec as P

REGULAR = 0.01

DEEP = 4
WIDE = 5
WINDOW = 4
MARGIN = 8
VMEM_LIMIT = 24 * 1024 * 1024


def call(kernel, outs, scratch=(), **specs):
    return pl.pallas_call(
        kernel,
        out_shape=outs,
        scratch_shapes=scratch,
        compiler_params=pltpu.CompilerParams(vmem_limit_bytes=VMEM_LIMIT),
        **specs,
    )


def f32(*shape):
    return jax.ShapeDtypeStruct(shape, jnp.float32)


def even(axis):
    return lax.rem(lax.axis_index(axis), 2) == 0


def face_planes(parts):
    for part in range(parts + 1):
        for number in range(DEEP if part < parts - 1 else DEEP - 1):
            yield part, number


def face_starts(part, parts, levels):
    return 0, levels - (DEEP if part < parts - 1 else DEEP - 1)


def pack_columns(
    flow_far, fluid_far, bed_far, thickness_far, mask_far,
    to_near, to_next, state, planes, flow, fluid, bed, thickness, mask, arrived,
):
    far = (flow_far, fluid_far, bed_far, thickness_far, mask_far)
    near = (flow, fluid, bed, thickness, mask)
    copies = [pltpu.make_async_copy(a, b, arrived.at[i]) for i, (a, b) in enumerate(zip(far, near, strict=True))]
    for copy in copies:
        copy.start()
    for copy in copies:
        copy.wait()
    parts, levels, columns, _ = flow.shape
    upward = even("gx")
    height = thickness[...]
    flat = (bed[...] + height, height, mask[...].astype(jnp.float32))
    place = 0

    def put(low, high):
        to_near[place : place + WIDE, :] = jnp.where(upward, high, low)
        to_next[place : place + WIDE, :] = jnp.where(upward, low, high)
        return place + WIDE

    for part in range(parts + 1):
        for level in range(levels):
            plane = flow.at[part, level] if part < parts else fluid.at[level]
            place = put(plane[:WIDE, :], plane[columns - WIDE :, :])
    for plane in flat:
        place = put(plane[:WIDE, :], plane[columns - WIDE :, :])
    lead = MARGIN + WINDOW
    for part in range(parts + 1):
        for level in range(levels):
            plane = flow.at[part, level] if part < parts else fluid.at[level]
            state[part, DEEP + level, lead : lead + columns, :] = plane[...]
    for number, plane in enumerate(flat):
        planes[number, lead : lead + columns, :] = plane


def unpaired(axis):
    place = lax.axis_index(axis)
    return (place == 0) | (place == lax.axis_size(axis) - 1)


def beside(near, next_, place, fluid_plane):
    inner = near[place : place + WIDE, :]
    beyond = next_[place : place + WIDE, :]
    if fluid_plane:
        beyond = jnp.where(unpaired("gx"), jnp.inf, beyond)
    return jnp.where(even("gx"), beyond, inner), jnp.where(even("gx"), inner, beyond)


def pack_levels(parts, levels, columns, state_in, planes_in, next_, near, state, planes, to_near, to_next):
    upward = even("gz")
    lead = MARGIN + WINDOW
    tail = lead + columns
    rows = columns + 2 * WINDOW
    for part in range(parts + 1):
        for level in range(levels):
            before, after = beside(near, next_, (part * levels + level) * WIDE, part == parts)
            state[part, DEEP + level, :, :] = state_in[part, DEEP + level]
            state[part, DEEP + level, lead - WIDE : lead, :] = before
            state[part, DEEP + level, tail : tail + WIDE, :] = after
    for number in range(planes.shape[0]):
        before, after = beside(near, next_, ((parts + 1) * levels + number) * WIDE, False)
        planes[number, :, :] = planes_in[number]
        planes[number, lead - WIDE : lead, :] = before
        planes[number, tail : tail + WIDE, :] = after
    for index, (part, number) in enumerate(face_planes(parts)):
        low, high = (DEEP + start + number for start in face_starts(part, parts, levels))
        spot = slice(index * rows, (index + 1) * rows)
        for out, level in ((to_near, jnp.where(upward, high, low)), (to_next, jnp.where(upward, low, high))):
            out[spot, :] = state[part, level, MARGIN : MARGIN + rows, :]


def along_y(field):
    lane = lax.broadcasted_iota(jnp.int32, field.shape, 1)
    end = field.shape[1] - 1
    upper = jnp.where(lane < end, pltpu.roll(field, end, 1), 0.0)
    lower = jnp.where(lane > 0, pltpu.roll(field, 1, 1), 0.0)
    return upper - lower


def evolve(state_in, planes, face_next, face_near, density, out, message, state, stress, extra, slopes, marks):
    parts, levels, columns, lanes = out.shape
    rows = columns + 2 * WINDOW
    deep = levels + 2 * DEEP
    win = slice(MARGIN, MARGIN + rows)
    ahead = slice(MARGIN + 1, MARGIN + rows + 1)
    behind = slice(MARGIN - 1, MARGIN + rows - 1)
    lowest = lax.axis_index("gz") == 0
    highest = lax.axis_index("gz") == lax.axis_size("gz") - 1
    upward = even("gz")

    for part in range(parts + 1):
        for level in range(levels):
            state[part, DEEP + level] = state_in[part, DEEP + level]
    for face, above in ((face_near, upward), (face_next, ~upward)):
        for index, (part, number) in enumerate(face_planes(parts)):
            plane = face[rows * index : rows * (index + 1), :]
            if part == parts and face is face_next:
                plane = jnp.where(unpaired("gz"), jnp.inf, plane)
            level = number + jnp.where(above, DEEP + levels, 0 if part < parts - 1 else 1)
            state[part, level, win, :] = plane

    slopes[0] = 4.0 * (planes[0, ahead, :] - planes[0, behind, :])
    slopes[1] = 4.0 * along_y(planes[0, win, :])
    kind = planes[2, win, :]
    ice = jnp.where(kind > 0.5, 1.0, 0.0)
    marks[0] = jnp.where(lowest, 0.0, ice)
    marks[1] = ice
    marks[2] = jnp.where(highest, 0.0, ice)
    marks[3] = jnp.zeros_like(ice)
    marks[4] = jnp.where(lowest & (kind > 0.5) & (kind < 1.5), 16.0, 0.0)

    def strain(k, carry):
        def across(part):
            return state[part, k, ahead, :] - state[part, k, behind, :]

        def upward(part):
            return state[part, k + 1, win, :] - state[part, k - 1, win, :]

        xx = across(0)
        yy = along_y(state[1, k, win, :])
        zz = upward(2)
        xy = along_y(state[0, k, win, :]) + across(1)
        xz = upward(0) + across(2)
        yz = upward(1) + along_y(state[2, k, win, :])
        second = 2.0 * (xx * xx + yy * yy + zz * zz) + (xy * xy + xz * xz + yz * yz)
        base = state[4, k, win, :] * (second * 0.0625 + REGULAR)
        root = jnp.exp2(jnp.log2(base) * (-1.0 / 3.0))
        pressure = state[3, k, win, :]
        push = 4.0 * pressure
        twice = 2.0 * root
        stress[0, k, win, :] = twice * xx - push
        stress[1, k, win, :] = twice * yy - push
        stress[2, k, win, :] = twice * zz - push
        stress[3, k, win, :] = root * xy
        stress[4, k, win, :] = root * xz
        stress[5, k, win, :] = root * yz
        extra[0, k] = 0.05 * (base * (root * root))
        extra[1, k] = pressure - (0.05 * root) * (xx + yy + zz)
        return carry

    def forces(k):
        def across(which):
            return stress[which, k, ahead, :] - stress[which, k, behind, :]

        def upward(which):
            return stress[which, k + 1, win, :] - stress[which, k - 1, win, :]

        def sideways(which):
            return along_y(stress[which, k, win, :])

        factor = extra[0, k]
        inside = marks[(k >= DEEP).astype(jnp.int32) + (k >= DEEP + levels).astype(jnp.int32)] > 0.5
        drag = marks[3 + (k == DEEP).astype(jnp.int32)]
        u = state[0, k, win, :]
        v = state[1, k, win, :]
        w = state[2, k, win, :]
        force_x = across(0) + sideways(3) + upward(4) - slopes[0] - drag * u
        force_y = across(3) + sideways(1) + upward(5) - slopes[1] - drag * v
        force_z = across(4) + sideways(5) + upward(2)
        return (
            jnp.where(inside, u + factor * force_x, 0.0),
            jnp.where(inside, v + factor * force_y, 0.0),
            jnp.where(inside, w + factor * force_z, 0.0),
            jnp.where(inside, extra[1, k], 0.0),
        )

    def first(k, carry):
        for part, value in enumerate(forces(k)):
            state[part, k, win, :] = value
        return carry

    own = slice(WINDOW, WINDOW + columns)

    def second(k, carry):
        values = forces(k)
        for part, value in enumerate(values):
            out[part, k - DEEP] = value[own, :]
        return carry[0] + values[0], carry[1] + values[1]

    lax.fori_loop(1, deep - 1, strain, 0)
    lax.fori_loop(2, deep - 2, first, 0)
    lax.fori_loop(3, deep - 3, strain, 0)
    nothing = jnp.zeros((rows, lanes), jnp.float32)
    sum_u, sum_v = lax.fori_loop(DEEP, deep - DEEP, second, (nothing, nothing))

    half = 0.5 / (levels * lax.axis_size("gz"))
    height = planes[1, win, :]
    slopes[0] = height * sum_u
    flux_y = along_y(height * sum_v)
    flux_x = slopes[0, WINDOW + 1 : WINDOW + columns + 1, :] - slopes[0, WINDOW - 1 : WINDOW + columns - 1, :]
    spread = half * (flux_x + flux_y[own, :])
    weight = jnp.sum(density[...], axis=0)
    for target in range(message.shape[0]):
        message[target, :columns, :] = spread
        message[target, columns:, :] = weight


def finish(message, density, thickness, smb, moved, grown, burden, out, sent):
    copy = pltpu.make_async_copy(moved, out, sent)
    copy.start()
    devices = message.shape[0]
    levels, columns, _ = density.shape
    place = lax.axis_index("gz")
    spread = message[0, :columns, :]
    over = jnp.where(place < 0, message[0, columns:, :], 0.0)
    for device in range(1, devices):
        spread = spread + message[device, :columns, :]
        over = over + jnp.where(place < device, message[device, columns:, :], 0.0)
    new = thickness[...] + 0.5 * (smb[...] - spread)
    grown[...] = new
    scaled = new * (1.0 / (levels * devices))
    for level in range(levels - 1, -1, -1):
        here = density[level]
        burden[level] = scaled * (over + 0.5 * here)
        over = over + here
    copy.wait()


def traded(to_near, to_next, axis):
    count = lax.axis_size(axis)
    pairs = [(i, i ^ 1) for i in range(count)]
    next_ = lax.ppermute(to_next, axis, [(i + 1, j + 1) for i, j in pairs[: count - 2]])
    near = lax.ppermute(to_near, axis, pairs)
    return near, next_


def body(flow, fluid, density, thickness, bed, smb, mask):
    parts, levels, columns, lanes = flow.shape
    rows = columns + 2 * WINDOW
    deep = levels + 2 * DEEP
    tall = rows + 2 * MARGIN
    side = f32(((parts + 1) * levels + 3) * WIDE, lanes)
    face = f32(((parts + 1) * DEEP - 2) * rows, lanes)
    wide = (parts + 1, deep, tall, lanes)
    flat = (3, tall, lanes)
    inputs = (flow, fluid, bed, thickness, mask)
    to_near, to_next, state, planes = call(
        pack_columns,
        (side, side, f32(*wide), f32(*flat)),
        in_specs=[pl.BlockSpec(memory_space=pltpu.HBM)] * len(inputs),
        scratch=[pltpu.VMEM(each.shape, each.dtype) for each in inputs] + [pltpu.SemaphoreType.DMA((len(inputs),))],
    )(*(pltpu.with_memory_space_constraint(each, pltpu.HBM) for each in inputs))
    near, next_ = traded(to_near, to_next, "gx")

    state, planes, to_near, to_next = call(
        functools.partial(pack_levels, parts, levels, columns),
        (f32(*wide), f32(*flat), face, face),
    )(state, planes, next_, near)
    face_near, face_next = traded(to_near, to_next, "gz")

    message = f32(lax.axis_size("gz"), 2 * columns, lanes)
    moved, message = call(
        evolve,
        (f32(*flow.shape), message),
        scratch=[
            pltpu.VMEM(wide, jnp.float32),
            pltpu.VMEM((6, deep, tall, lanes), jnp.float32),
            pltpu.VMEM((2, deep, rows, lanes), jnp.float32),
            pltpu.VMEM((2, rows, lanes), jnp.float32),
            pltpu.VMEM((5, rows, lanes), jnp.float32),
        ],
    )(state, planes, face_next, face_near, density)
    message = lax.all_to_all(message, "gz", split_axis=0, concat_axis=0, tiled=True)
    inner = pl.BlockSpec(memory_space=pltpu.VMEM)
    grown, burden, moved = call(
        finish,
        (f32(columns, lanes), f32(*density.shape), f32(*flow.shape)),
        out_specs=[inner, inner, pl.BlockSpec(memory_space=pltpu.HBM)],
        scratch=[pltpu.SemaphoreType.DMA],
    )(message, density, thickness, smb, moved)
    return moved, grown, burden


def solution(mesh):
    level_split = P("gz", "gx", None)
    flat = P("gx", None)
    return jax.shard_map(
        body,
        mesh=mesh,
        in_specs=(P(None, "gz", "gx", None), level_split, level_split, flat, flat, flat, flat),
        out_specs=(P(None, "gz", "gx", None), flat, level_split),
        check_vma=False,
    )
```

```python
import functools

import jax
import jax.numpy as jnp
from jax import lax
from jax.experimental import pallas as pl
from jax.experimental.pallas import tpu as pltpu
from jax.sharding import PartitionSpec as P

REGULAR = 0.01

DEEP = 4
WIDE = 5
WINDOW = 4
MARGIN = 8
VMEM_LIMIT = 24 * 1024 * 1024
WIDEN_COST = 5_000_000_000
STORE_COST = 5_000_000


def call(kernel, outs, scratch=(), **specs):
    return pl.pallas_call(
        kernel,
        out_shape=outs,
        scratch_shapes=scratch,
        compiler_params=pltpu.CompilerParams(vmem_limit_bytes=VMEM_LIMIT),
        **specs,
    )


def f32(*shape):
    return jax.ShapeDtypeStruct(shape, jnp.float32)


def even(axis):
    return lax.rem(lax.axis_index(axis), 2) == 0


def face_planes(parts):
    for part in range(parts + 1):
        for number in range(DEEP if part < parts - 1 else DEEP - 1):
            yield part, number


def face_starts(part, parts, levels):
    return 0, levels - (DEEP if part < parts - 1 else DEEP - 1)


def prepare(
    flow_far, fluid_far, bed_far, thickness_far, mask_far,
    to_near, to_next, face_near, face_next, state, planes, flow, fluid, bed, thickness, mask, arrived,
):
    far = (flow_far, fluid_far, bed_far, thickness_far, mask_far)
    near = (flow, fluid, bed, thickness, mask)
    copies = [pltpu.make_async_copy(a, b, arrived.at[i]) for i, (a, b) in enumerate(zip(far, near, strict=True))]
    for copy in copies:
        copy.start()
    for copy in copies:
        copy.wait()
    parts, levels, columns, _ = flow.shape
    upward = even("gx")
    height = thickness[...]
    flat = (bed[...] + height, height, mask[...].astype(jnp.float32))
    place = 0

    def put(low, high):
        to_near[place : place + WIDE, :] = jnp.where(upward, high, low)
        to_next[place : place + WIDE, :] = jnp.where(upward, low, high)
        return place + WIDE

    for part in range(parts + 1):
        for level in range(levels):
            plane = flow.at[part, level] if part < parts else fluid.at[level]
            place = put(plane[:WIDE, :], plane[columns - WIDE :, :])
    for plane in flat:
        place = put(plane[:WIDE, :], plane[columns - WIDE :, :])
    above = even("gz")
    for index, (part, number) in enumerate(face_planes(parts)):
        low, high = (start + number for start in face_starts(part, parts, levels))
        whole = flow.at[part] if part < parts else fluid
        spot = slice(index * columns, (index + 1) * columns)
        face_near[spot, :] = whole[jnp.where(above, high, low)]
        face_next[spot, :] = whole[jnp.where(above, low, high)]
    lead = MARGIN + WINDOW
    for part in range(parts + 1):
        for level in range(levels):
            plane = flow.at[part, level] if part < parts else fluid.at[level]
            state[part, DEEP + level, lead : lead + columns, :] = plane[...]
    for number, plane in enumerate(flat):
        planes[number, lead : lead + columns, :] = plane


def unpaired(axis):
    place = lax.axis_index(axis)
    return (place == 0) | (place == lax.axis_size(axis) - 1)


def beside(near, next_, place, fluid_plane):
    inner = near[place : place + WIDE, :]
    beyond = next_[place : place + WIDE, :]
    if fluid_plane:
        beyond = jnp.where(unpaired("gx"), jnp.inf, beyond)
    return jnp.where(even("gx"), beyond, inner), jnp.where(even("gx"), inner, beyond)


def pack_corners(parts, levels, next_, near, to_near, to_next):
    upward = even("gz")
    for index, (part, number) in enumerate(face_planes(parts)):
        low, high = (
            beside(near, next_, (part * levels + start + number) * WIDE, part == parts)
            for start in face_starts(part, parts, levels)
        )
        for side, cut in ((0, slice(WIDE - WINDOW, WIDE)), (1, slice(0, WINDOW))):
            spot = slice((2 * index + side) * WINDOW, (2 * index + side + 1) * WINDOW)
            to_near[spot, :] = jnp.where(upward, high[side], low[side])[cut, :]
            to_next[spot, :] = jnp.where(upward, low[side], high[side])[cut, :]


def widen(parts, levels, columns, state_in, planes_in, next_, near, state, planes):
    lead = MARGIN + WINDOW
    tail = lead + columns
    for part in range(parts + 1):
        for level in range(levels):
            before, after = beside(near, next_, (part * levels + level) * WIDE, part == parts)
            state[part, DEEP + level, :, :] = state_in[part, DEEP + level]
            state[part, DEEP + level, lead - WIDE : lead, :] = before
            state[part, DEEP + level, tail : tail + WIDE, :] = after
    for number in range(planes.shape[0]):
        before, after = beside(near, next_, ((parts + 1) * levels + number) * WIDE, False)
        planes[number, :, :] = planes_in[number]
        planes[number, lead - WIDE : lead, :] = before
        planes[number, tail : tail + WIDE, :] = after


def along_y(field):
    lane = lax.broadcasted_iota(jnp.int32, field.shape, 1)
    end = field.shape[1] - 1
    upper = jnp.where(lane < end, pltpu.roll(field, end, 1), 0.0)
    lower = jnp.where(lane > 0, pltpu.roll(field, 1, 1), 0.0)
    return upper - lower


def evolve(
    state_in, planes, edge_next, edge_near, face_next, face_near, density,
    out, message, state, stress, extra, slopes, marks,
):
    parts, levels, columns, lanes = out.shape
    rows = columns + 2 * WINDOW
    deep = levels + 2 * DEEP
    win = slice(MARGIN, MARGIN + rows)
    ahead = slice(MARGIN + 1, MARGIN + rows + 1)
    behind = slice(MARGIN - 1, MARGIN + rows - 1)
    lowest = lax.axis_index("gz") == 0
    highest = lax.axis_index("gz") == lax.axis_size("gz") - 1
    upward = even("gz")
    lead = MARGIN + WINDOW
    tail = lead + columns

    for part in range(parts + 1):
        for level in range(levels):
            state[part, DEEP + level] = state_in[part, DEEP + level]
    for face, edge, above in ((face_near, edge_near, upward), (face_next, edge_next, ~upward)):
        for index, (part, number) in enumerate(face_planes(parts)):
            middle = face[columns * index : columns * (index + 1), :]
            sides = edge[2 * WINDOW * index : 2 * WINDOW * (index + 1), :]
            if part == parts and face is face_next:
                middle, sides = (jnp.where(unpaired("gz"), jnp.inf, each) for each in (middle, sides))
            level = number + jnp.where(above, DEEP + levels, 0 if part < parts - 1 else 1)
            state[part, level, lead - WINDOW : lead, :] = sides[:WINDOW, :]
            state[part, level, lead:tail, :] = middle
            state[part, level, tail : tail + WINDOW, :] = sides[WINDOW:, :]

    slopes[0] = 4.0 * (planes[0, ahead, :] - planes[0, behind, :])
    slopes[1] = 4.0 * along_y(planes[0, win, :])
    kind = planes[2, win, :]
    ice = jnp.where(kind > 0.5, 1.0, 0.0)
    marks[0] = jnp.where(lowest, 0.0, ice)
    marks[1] = ice
    marks[2] = jnp.where(highest, 0.0, ice)
    marks[3] = jnp.zeros_like(ice)
    marks[4] = jnp.where(lowest & (kind > 0.5) & (kind < 1.5), 16.0, 0.0)

    def strain(k, carry):
        def across(part):
            return state[part, k, ahead, :] - state[part, k, behind, :]

        def upward(part):
            return state[part, k + 1, win, :] - state[part, k - 1, win, :]

        xx = across(0)
        yy = along_y(state[1, k, win, :])
        zz = upward(2)
        xy = along_y(state[0, k, win, :]) + across(1)
        xz = upward(0) + across(2)
        yz = upward(1) + along_y(state[2, k, win, :])
        second = 2.0 * (xx * xx + yy * yy + zz * zz) + (xy * xy + xz * xz + yz * yz)
        base = state[4, k, win, :] * (second * 0.0625 + REGULAR)
        root = jnp.exp2(jnp.log2(base) * (-1.0 / 3.0))
        pressure = state[3, k, win, :]
        push = 4.0 * pressure
        twice = 2.0 * root
        stress[0, k, win, :] = twice * xx - push
        stress[1, k, win, :] = twice * yy - push
        stress[2, k, win, :] = twice * zz - push
        stress[3, k, win, :] = root * xy
        stress[4, k, win, :] = root * xz
        stress[5, k, win, :] = root * yz
        extra[0, k] = 0.05 * (base * (root * root))
        extra[1, k] = pressure - (0.05 * root) * (xx + yy + zz)
        return carry

    def forces(k):
        def across(which):
            return stress[which, k, ahead, :] - stress[which, k, behind, :]

        def upward(which):
            return stress[which, k + 1, win, :] - stress[which, k - 1, win, :]

        def sideways(which):
            return along_y(stress[which, k, win, :])

        factor = extra[0, k]
        inside = marks[(k >= DEEP).astype(jnp.int32) + (k >= DEEP + levels).astype(jnp.int32)] > 0.5
        drag = marks[3 + (k == DEEP).astype(jnp.int32)]
        u = state[0, k, win, :]
        v = state[1, k, win, :]
        w = state[2, k, win, :]
        force_x = across(0) + sideways(3) + upward(4) - slopes[0] - drag * u
        force_y = across(3) + sideways(1) + upward(5) - slopes[1] - drag * v
        force_z = across(4) + sideways(5) + upward(2)
        return (
            jnp.where(inside, u + factor * force_x, 0.0),
            jnp.where(inside, v + factor * force_y, 0.0),
            jnp.where(inside, w + factor * force_z, 0.0),
            jnp.where(inside, extra[1, k], 0.0),
        )

    def first(k, carry):
        for part, value in enumerate(forces(k)):
            state[part, k, win, :] = value
        return carry

    own = slice(WINDOW, WINDOW + columns)

    def second(k, carry):
        values = forces(k)
        for part, value in enumerate(values):
            out[part, k - DEEP] = value[own, :]
        return carry[0] + values[0], carry[1] + values[1]

    lax.fori_loop(1, deep - 1, strain, 0, unroll=True)
    lax.fori_loop(2, deep - 2, first, 0, unroll=True)
    lax.fori_loop(3, deep - 3, strain, 0, unroll=True)
    nothing = jnp.zeros((rows, lanes), jnp.float32)
    sum_u, sum_v = lax.fori_loop(DEEP, deep - DEEP, second, (nothing, nothing), unroll=True)

    half = 0.5 / (levels * lax.axis_size("gz"))
    height = planes[1, win, :]
    slopes[0] = height * sum_u
    flux_y = along_y(height * sum_v)
    flux_x = slopes[0, WINDOW + 1 : WINDOW + columns + 1, :] - slopes[0, WINDOW - 1 : WINDOW + columns - 1, :]
    spread = half * (flux_x + flux_y[own, :])
    weight = jnp.sum(density[...], axis=0)
    for target in range(message.shape[0]):
        message[target, :columns, :] = spread
        message[target, columns:, :] = weight


def store(moved, out, sent):
    copy = pltpu.make_async_copy(moved, out, sent)
    copy.start()
    copy.wait()


def finish(message, density, thickness, smb, grown, burden):
    devices = message.shape[0]
    levels, columns, _ = density.shape
    place = lax.axis_index("gz")
    spread = message[0, :columns, :]
    over = jnp.where(place < 0, message[0, columns:, :], 0.0)
    for device in range(1, devices):
        spread = spread + message[device, :columns, :]
        over = over + jnp.where(place < device, message[device, columns:, :], 0.0)
    new = thickness[...] + 0.5 * (smb[...] - spread)
    grown[...] = new
    scaled = new * (1.0 / (levels * devices))
    for level in range(levels - 1, -1, -1):
        here = density[level]
        burden[level] = scaled * (over + 0.5 * here)
        over = over + here


def traded(to_near, to_next, axis):
    count = lax.axis_size(axis)
    pairs = [(i, i ^ 1) for i in range(count)]
    next_ = lax.ppermute(to_next, axis, [(i + 1, j + 1) for i, j in pairs[: count - 2]])
    near = lax.ppermute(to_near, axis, pairs)
    return near, next_


def body(flow, fluid, density, thickness, bed, smb, mask):
    parts, levels, columns, lanes = flow.shape
    rows = columns + 2 * WINDOW
    deep = levels + 2 * DEEP
    tall = rows + 2 * MARGIN
    side = f32(((parts + 1) * levels + 3) * WIDE, lanes)
    faces = (parts + 1) * DEEP - 2
    face = f32(faces * columns, lanes)
    edge = f32(faces * 2 * WINDOW, lanes)
    wide = (parts + 1, deep, tall, lanes)
    flat = (3, tall, lanes)
    inputs = (flow, fluid, bed, thickness, mask)
    to_near, to_next, face_near, face_next, state, planes = call(
        prepare,
        (side, side, face, face, f32(*wide), f32(*flat)),
        in_specs=[pl.BlockSpec(memory_space=pltpu.HBM)] * len(inputs),
        scratch=[pltpu.VMEM(each.shape, each.dtype) for each in inputs] + [pltpu.SemaphoreType.DMA((len(inputs),))],
    )(*(pltpu.with_memory_space_constraint(each, pltpu.HBM) for each in inputs))
    near, next_ = traded(to_near, to_next, "gx")
    face_near, face_next = traded(face_near, face_next, "gz")
    to_near, to_next = call(functools.partial(pack_corners, parts, levels), (edge, edge))(next_, near)
    edge_near, edge_next = traded(to_near, to_next, "gz")
    state, planes = call(
        functools.partial(widen, parts, levels, columns),
        (f32(*wide), f32(*flat)),
        cost_estimate=pl.CostEstimate(flops=WIDEN_COST, bytes_accessed=WIDEN_COST, transcendentals=0),
    )(state, planes, next_, near)

    message = f32(lax.axis_size("gz"), 2 * columns, lanes)
    moved, message = call(
        evolve,
        (f32(*flow.shape), message),
        scratch=[
            pltpu.VMEM(wide, jnp.float32),
            pltpu.VMEM((6, deep, tall, lanes), jnp.float32),
            pltpu.VMEM((2, deep, rows, lanes), jnp.float32),
            pltpu.VMEM((2, rows, lanes), jnp.float32),
            pltpu.VMEM((5, rows, lanes), jnp.float32),
        ],
    )(state, planes, edge_next, edge_near, face_next, face_near, density)
    message = lax.all_to_all(message, "gz", split_axis=0, concat_axis=0, tiled=True)
    moved = call(
        store,
        f32(*flow.shape),
        out_specs=pl.BlockSpec(memory_space=pltpu.HBM),
        scratch=[pltpu.SemaphoreType.DMA],
        cost_estimate=pl.CostEstimate(flops=0, bytes_accessed=STORE_COST, transcendentals=0),
    )(moved)
    grown, burden = call(finish, (f32(columns, lanes), f32(*density.shape)))(message, density, thickness, smb)
    return moved, grown, burden


def solution(mesh):
    level_split = P("gz", "gx", None)
    flat = P("gx", None)
    return jax.shard_map(
        body,
        mesh=mesh,
        in_specs=(P(None, "gz", "gx", None), level_split, level_split, flat, flat, flat, flat),
        out_specs=(P(None, "gz", "gx", None), flat, level_split),
        check_vma=False,
    )
```

```python
import jax
import jax.numpy as jnp
from jax import lax
from jax.experimental import pallas as pl
from jax.experimental.pallas import tpu as pltpu
from jax.sharding import PartitionSpec as P

REGULAR = 0.01

DEEP = 4
WIDE = 5
WINDOW = 4
MARGIN = 8
VMEM_LIMIT = 24 * 1024 * 1024
INNER_COST = 5_000_000_000
STORE_COST = 5_000_000


def call(kernel, outs, scratch=(), **specs):
    return pl.pallas_call(
        kernel,
        out_shape=outs,
        scratch_shapes=scratch,
        compiler_params=pltpu.CompilerParams(vmem_limit_bytes=VMEM_LIMIT),
        **specs,
    )


def f32(*shape):
    return jax.ShapeDtypeStruct(shape, jnp.float32)


def even(axis):
    return lax.rem(lax.axis_index(axis), 2) == 0


def face_planes(parts):
    for part in range(parts + 1):
        for number in range(DEEP if part < parts - 1 else DEEP - 1):
            yield part, number


def face_starts(part, parts, levels):
    return 0, levels - (DEEP if part < parts - 1 else DEEP - 1)


def prepare(
    flow_far, fluid_far, bed_far, thickness_far, mask_far, density_far,
    to_near, to_next, to_level, state, planes, weight, flow, fluid, bed, thickness, mask, density, arrived,
):
    far = (flow_far, fluid_far, bed_far, thickness_far, mask_far, density_far)
    near = (flow, fluid, bed, thickness, mask, density)
    copies = [pltpu.make_async_copy(a, b, arrived.at[i]) for i, (a, b) in enumerate(zip(far, near, strict=True))]
    for copy in copies:
        copy.start()
    for copy in copies:
        copy.wait()
    parts, levels, columns, _ = flow.shape
    upward = even("gx")
    height = thickness[...]
    flat = (bed[...] + height, height, mask[...].astype(jnp.float32))
    place = 0

    def put(low, high):
        to_near[place : place + WIDE, :] = jnp.where(upward, high, low)
        to_next[place : place + WIDE, :] = jnp.where(upward, low, high)
        return place + WIDE

    for part in range(parts + 1):
        for level in range(levels):
            plane = flow.at[part, level] if part < parts else fluid.at[level]
            place = put(plane[:WIDE, :], plane[columns - WIDE :, :])
    for plane in flat:
        place = put(plane[:WIDE, :], plane[columns - WIDE :, :])
    above = even("gz")
    for index, (part, number) in enumerate(face_planes(parts)):
        low, high = (start + number for start in face_starts(part, parts, levels))
        whole = flow.at[part] if part < parts else fluid
        spot = slice(index * columns, (index + 1) * columns)
        to_level[spot, :] = whole[jnp.where(above, low, high)]
    lead = MARGIN + WINDOW
    for part in range(parts + 1):
        for level in range(levels):
            plane = flow.at[part, level] if part < parts else fluid.at[level]
            state[part, level, lead : lead + columns, :] = plane[...]
    for number, plane in enumerate(flat):
        planes[number, lead : lead + columns, :] = plane
    weight[...] = jnp.sum(density[...], axis=0)


def unpaired(axis):
    place = lax.axis_index(axis)
    return (place == 0) | (place == lax.axis_size(axis) - 1)


def beside(near, next_, place, fluid_plane):
    inner = near[place : place + WIDE, :]
    beyond = next_[place : place + WIDE, :]
    if fluid_plane:
        beyond = jnp.where(unpaired("gx"), jnp.inf, beyond)
    return jnp.where(even("gx"), beyond, inner), jnp.where(even("gx"), inner, beyond)


def widen(state_in, planes_in, weight, next_, near, state, planes, to_next, to_near):
    parts, levels, tall, _ = state_in.shape
    parts -= 1
    rows = tall - 2 * MARGIN
    lead = MARGIN + WINDOW
    tail = MARGIN + rows - WINDOW
    upward = even("gz")
    for part in range(parts + 1):
        for level in range(levels):
            before, after = beside(near, next_, (part * levels + level) * WIDE, part == parts)
            state[part, level, :, :] = state_in[part, level]
            state[part, level, lead - WIDE : lead, :] = before
            state[part, level, tail : tail + WIDE, :] = after
    for number in range(planes.shape[0]):
        before, after = beside(near, next_, ((parts + 1) * levels + number) * WIDE, False)
        planes[number, :, :] = planes_in[number]
        planes[number, lead - WIDE : lead, :] = before
        planes[number, tail : tail + WIDE, :] = after
    count = 0
    for index, (part, number) in enumerate(face_planes(parts)):
        low, high = (start + number for start in face_starts(part, parts, levels))
        to_near[index * rows : (index + 1) * rows, :] = state[
            part, jnp.where(upward, high, low), MARGIN : MARGIN + rows, :
        ]
        level = jnp.where(upward, low, high)
        spot = 2 * WINDOW * index
        to_next[spot : spot + WINDOW, :] = state[part, level, MARGIN:lead, :]
        to_next[spot + WINDOW : spot + 2 * WINDOW, :] = state[part, level, tail : tail + WINDOW, :]
        count = index + 1
    to_near[count * rows :, :] = weight[...]


def along_y(field):
    lane = lax.broadcasted_iota(jnp.int32, field.shape, 1)
    end = field.shape[1] - 1
    upper = jnp.where(lane < end, pltpu.roll(field, end, 1), 0.0)
    lower = jnp.where(lane > 0, pltpu.roll(field, 1, 1), 0.0)
    return upper - lower


def window(rows):
    return tuple(slice(MARGIN + shift, MARGIN + shift + rows) for shift in (0, 1, -1))


def strain(rows, cells, k, stress, extra):
    win, ahead, behind = window(rows)

    def across(part):
        return cells(part, k)[ahead, :] - cells(part, k)[behind, :]

    def upward(part):
        return cells(part, k + 1)[win, :] - cells(part, k - 1)[win, :]

    def sideways(part):
        return along_y(cells(part, k)[win, :])

    xx = across(0)
    yy = sideways(1)
    zz = upward(2)
    xy = sideways(0) + across(1)
    xz = upward(0) + across(2)
    yz = upward(1) + sideways(2)
    second = 2.0 * (xx * xx + yy * yy + zz * zz) + (xy * xy + xz * xz + yz * yz)
    base = cells(4, k)[win, :] * (second * 0.0625 + REGULAR)
    root = jnp.exp2(jnp.log2(base) * (-1.0 / 3.0))
    pressure = cells(3, k)[win, :]
    push = 4.0 * pressure
    twice = 2.0 * root
    stress(0, k)[win, :] = twice * xx - push
    stress(1, k)[win, :] = twice * yy - push
    stress(2, k)[win, :] = twice * zz - push
    stress(3, k)[win, :] = root * xy
    stress(4, k)[win, :] = root * xz
    stress(5, k)[win, :] = root * yz
    extra(0, k)[...] = 0.05 * (base * (root * root))
    extra(1, k)[...] = pressure - (0.05 * root) * (xx + yy + zz)


def moved_on(rows, cells, stress, extra, k, slopes, ice, drag):
    win, ahead, behind = window(rows)

    def across(which):
        return stress(which, k)[ahead, :] - stress(which, k)[behind, :]

    def upward(which):
        return stress(which, k + 1)[win, :] - stress(which, k - 1)[win, :]

    def sideways(which):
        return along_y(stress(which, k)[win, :])

    factor = extra(0, k)[...]
    inside = ice[...] > 0.5
    u, v, w = (cells(part, k)[win, :] for part in range(3))
    force_x = across(0) + sideways(3) + upward(4) - slopes[0]
    force_y = across(3) + sideways(1) + upward(5) - slopes[1]
    force_z = across(4) + sideways(5) + upward(2)
    if drag is not None:
        force_x = force_x - drag[...] * u
        force_y = force_y - drag[...] * v
    return (
        jnp.where(inside, u + factor * force_x, 0.0),
        jnp.where(inside, v + factor * force_y, 0.0),
        jnp.where(inside, w + factor * force_z, 0.0),
        jnp.where(inside, extra(1, k)[...], 0.0),
    )


def shared(rows, planes, slopes, marks):
    win, ahead, behind = window(rows)
    lowest = lax.axis_index("gz") == 0
    highest = lax.axis_index("gz") == lax.axis_size("gz") - 1
    slopes[0] = 4.0 * (planes[0, ahead, :] - planes[0, behind, :])
    slopes[1] = 4.0 * along_y(planes[0, win, :])
    kind = planes[2, win, :]
    ice = jnp.where(kind > 0.5, 1.0, 0.0)
    marks[0] = jnp.where(lowest, 0.0, ice)
    marks[1] = ice
    marks[2] = jnp.where(highest, 0.0, ice)
    marks[3] = jnp.where(lowest & (kind > 0.5) & (kind < 1.5), 16.0, 0.0)


def inner(state, planes, stress, extra, fresh, slopes, marks):
    levels, tall, _ = state.shape[1:]
    rows = tall - 2 * MARGIN
    win, _, _ = window(rows)

    def cells(part, k):
        return state.at[part, k - DEEP]

    def stresses(which, k):
        return stress.at[which, k - DEEP - 1]

    def extras(which, k):
        return extra.at[which, k - DEEP - 1]

    shared(rows, planes, slopes, marks)
    for k in range(DEEP + 1, DEEP + levels - 1):
        strain(rows, cells, k, stresses, extras)
    for k in range(DEEP + 2, DEEP + levels - 2):
        for part, value in enumerate(moved_on(rows, cells, stresses, extras, k, slopes, marks.at[1], None)):
            fresh[part, k - DEEP - 2, win, :] = value


def evolve(
    own, planes, weight, stress_in, extra_in, fresh, face_next, edge_next, face_near,
    out, message, beyond, later, stress, extra, slopes, marks,
):
    parts, levels, columns, lanes = out.shape
    rows = columns + 2 * WINDOW
    deep = levels + 2 * DEEP
    win, _, _ = window(rows)
    upward = even("gz")
    lead = MARGIN + WINDOW
    tail = lead + columns

    count = 0
    for index, (part, number) in enumerate(face_planes(parts)):
        lower = 0 if part < parts - 1 else 1
        whole = face_near[rows * index : rows * (index + 1), :]
        beyond[part, number + jnp.where(upward, DEEP, lower), win, :] = whole
        middle = face_next[columns * index : columns * (index + 1), :]
        sides = edge_next[2 * WINDOW * index : 2 * WINDOW * (index + 1), :]
        if part == parts:
            middle, sides = (jnp.where(unpaired("gz"), jnp.inf, each) for each in (middle, sides))
        level = number + jnp.where(upward, lower, DEEP)
        beyond[part, level, lead - WINDOW : lead, :] = sides[:WINDOW, :]
        beyond[part, level, lead:tail, :] = middle
        beyond[part, level, tail : tail + WINDOW, :] = sides[WINDOW:, :]
        count = index + 1
    shared(rows, planes, slopes, marks)

    def before(part, k):
        if DEEP <= k < DEEP + levels:
            return own.at[part, k - DEEP]
        return beyond.at[part, k if k < DEEP else k - levels]

    def between(part, k):
        if part == parts:
            return before(part, k)
        if DEEP + 2 <= k < DEEP + levels - 2:
            return fresh.at[part, k - DEEP - 2]
        return later.at[part, k]

    def is_inner(k):
        return DEEP + 1 <= k < DEEP + levels - 1

    def stress_one(which, k):
        return stress_in.at[which, k - DEEP - 1] if is_inner(k) else stress.at[which, k]

    def extra_one(which, k):
        return extra_in.at[which, k - DEEP - 1] if is_inner(k) else extra.at[which, k]

    def stress_two(which, k):
        return stress.at[which, k]

    def extra_two(which, k):
        return extra.at[which, k]

    for k in range(1, deep - 1):
        if not is_inner(k):
            strain(rows, before, k, stress_one, extra_one)
    for k in range(2, deep - 2):
        if DEEP + 2 <= k < DEEP + levels - 2:
            continue
        ice = marks.at[0 if k < DEEP else 1 if k < DEEP + levels else 2]
        drag = marks.at[3] if k == DEEP else None
        for part, value in enumerate(moved_on(rows, before, stress_one, extra_one, k, slopes, ice, drag)):
            later[part, k, win, :] = value
    for k in range(3, deep - 3):
        strain(rows, between, k, stress_two, extra_two)
    cut = slice(WINDOW, WINDOW + columns)
    sum_u = sum_v = jnp.zeros((rows, lanes), jnp.float32)
    for k in range(DEEP, DEEP + levels):
        drag = marks.at[3] if k == DEEP else None
        values = moved_on(rows, between, stress_two, extra_two, k, slopes, marks.at[1], drag)
        for part, value in enumerate(values):
            out[part, k - DEEP] = value[cut, :]
        sum_u, sum_v = sum_u + values[0], sum_v + values[1]

    half = 0.5 / (levels * lax.axis_size("gz"))
    height = planes[1, win, :]
    slopes[0] = height * sum_u
    flux_y = along_y(height * sum_v)
    flux_x = slopes[0, WINDOW + 1 : WINDOW + columns + 1, :] - slopes[0, WINDOW - 1 : WINDOW + columns - 1, :]
    spread = half * (flux_x + flux_y[cut, :])
    both = weight[...] + face_near[count * rows :, :]
    part_of_both = jnp.where(upward, both[: columns // 2, :], both[columns // 2 :, :])
    for target in range(message.shape[0]):
        message[target, :columns, :] = spread
        message[target, columns:, :] = part_of_both


def store(moved, out, sent):
    copy = pltpu.make_async_copy(moved, out, sent)
    copy.start()
    copy.wait()


def finish(message, density, thickness, smb, other, grown, burden):
    devices = message.shape[0]
    levels, columns, _ = density.shape
    count = other.shape[0] - columns
    place = lax.axis_index("gz")
    spread = message[0, :columns, :]
    for device in range(1, devices):
        spread = spread + message[device, :columns, :]
    over = jnp.where(even("gz"), other[count:, :], 0.0)
    for device in range(2, devices, 2):
        both = jnp.concatenate([message[device, columns:, :], message[device + 1, columns:, :]], axis=0)
        over = over + jnp.where(place < device, both, 0.0)
    new = thickness[...] + 0.5 * (smb[...] - spread)
    grown[...] = new
    scaled = new * (1.0 / (levels * devices))
    for level in range(levels - 1, -1, -1):
        here = density[level]
        burden[level] = scaled * (over + 0.5 * here)
        over = over + here


def pairs_of(axis):
    near = [(i, i ^ 1) for i in range(lax.axis_size(axis))]
    return near, [(i + 1, j + 1) for i, j in near[:-2]]


def body(flow, fluid, density, thickness, bed, smb, mask):
    parts, levels, columns, lanes = flow.shape
    rows = columns + 2 * WINDOW
    deep = levels + 2 * DEEP
    tall = rows + 2 * MARGIN
    near_x, next_x = pairs_of("gx")
    near_z, next_z = pairs_of("gz")

    side = f32(((parts + 1) * levels + 3) * WIDE, lanes)
    faces = (parts + 1) * DEEP - 2
    wide = f32(parts + 1, levels, tall, lanes)
    flat = f32(3, tall, lanes)
    plane = f32(columns, lanes)
    inputs = (flow, fluid, bed, thickness, mask, density)
    to_near, to_next, to_level, state, planes, weight = call(
        prepare,
        (side, side, f32(faces * columns, lanes), wide, flat, plane),
        in_specs=[pl.BlockSpec(memory_space=pltpu.HBM)] * len(inputs),
        scratch=[pltpu.VMEM(each.shape, each.dtype) for each in inputs] + [pltpu.SemaphoreType.DMA((len(inputs),))],
    )(*(pltpu.with_memory_space_constraint(each, pltpu.HBM) for each in inputs))
    next_ = lax.ppermute(to_next, "gx", next_x)
    near = lax.ppermute(to_near, "gx", near_x)
    face_next = lax.ppermute(to_level, "gz", next_z)

    state, planes, to_next, to_near = call(
        widen, (wide, flat, f32(faces * 2 * WINDOW, lanes), f32(faces * rows + columns, lanes))
    )(state, planes, weight, next_, near)
    edge_next = lax.ppermute(to_next, "gz", next_z)
    face_near = lax.ppermute(to_near, "gz", near_z)

    stress, extra, fresh = call(
        inner,
        (f32(6, levels - 2, tall, lanes), f32(2, levels - 2, rows, lanes), f32(parts, levels - 4, tall, lanes)),
        scratch=[pltpu.VMEM((2, rows, lanes), jnp.float32), pltpu.VMEM((4, rows, lanes), jnp.float32)],
        cost_estimate=pl.CostEstimate(flops=INNER_COST, bytes_accessed=INNER_COST, transcendentals=0),
    )(state, planes)

    message = f32(lax.axis_size("gz"), columns + columns // 2, lanes)
    moved, message = call(
        evolve,
        (f32(*flow.shape), message),
        scratch=[
            pltpu.VMEM((parts + 1, 2 * DEEP, tall, lanes), jnp.float32),
            pltpu.VMEM((parts, deep, tall, lanes), jnp.float32),
            pltpu.VMEM((6, deep, tall, lanes), jnp.float32),
            pltpu.VMEM((2, deep, rows, lanes), jnp.float32),
            pltpu.VMEM((2, rows, lanes), jnp.float32),
            pltpu.VMEM((4, rows, lanes), jnp.float32),
        ],
    )(state, planes, weight, stress, extra, fresh, face_next, edge_next, face_near)
    message = lax.all_to_all(message, "gz", split_axis=0, concat_axis=0, tiled=True)
    moved = call(
        store,
        f32(*flow.shape),
        out_specs=pl.BlockSpec(memory_space=pltpu.HBM),
        scratch=[pltpu.SemaphoreType.DMA],
        cost_estimate=pl.CostEstimate(flops=0, bytes_accessed=STORE_COST, transcendentals=0),
    )(moved)
    grown, burden = call(finish, (plane, f32(*density.shape)))(message, density, thickness, smb, face_near)
    return moved, grown, burden


def solution(mesh):
    level_split = P("gz", "gx", None)
    flat = P("gx", None)
    return jax.shard_map(
        body,
        mesh=mesh,
        in_specs=(P(None, "gz", "gx", None), level_split, level_split, flat, flat, flat, flat),
        out_specs=(P(None, "gz", "gx", None), flat, level_split),
        check_vma=False,
    )
```

```python
import jax
import jax.numpy as jnp
from jax import lax
from jax.experimental import pallas as pl
from jax.experimental.pallas import tpu as pltpu
from jax.sharding import PartitionSpec as P

REGULAR = 0.01

DEEP = 4
WIDE = 5
WINDOW = 4
FLAT = (4, 1, 3)
MARGIN = 8
VMEM_LIMIT = 24 * 1024 * 1024
INNER_COST = 5_000_000_000


def call(kernel, outs, scratch=(), **specs):
    return pl.pallas_call(
        kernel,
        out_shape=outs,
        scratch_shapes=scratch,
        compiler_params=pltpu.CompilerParams(vmem_limit_bytes=VMEM_LIMIT),
        **specs,
    )


def f32(*shape):
    return jax.ShapeDtypeStruct(shape, jnp.float32)


def side_planes(parts, levels):
    place = 0
    for part in range(parts + 1):
        for level in range(levels):
            width = WIDE if part < parts - 1 else WINDOW
            yield part, level, width, place
            place += width
    for number, width in enumerate(FLAT):
        yield parts + 1, number, width, place
        place += width


def even(axis):
    return lax.rem(lax.axis_index(axis), 2) == 0


def face_planes(parts):
    for part in range(parts + 1):
        for number in range(DEEP if part < parts - 1 else DEEP - 1):
            yield part, number


def face_starts(part, parts, levels):
    return 0, levels - (DEEP if part < parts - 1 else DEEP - 1)


def prepare(
    flow_far, fluid_far, bed_far, thickness_far, mask_far, density_far,
    to_near, to_next, to_level, state, planes, weight, flow, fluid, bed, thickness, mask, density, arrived,
):
    far = (flow_far, fluid_far, bed_far, thickness_far, mask_far, density_far)
    near = (flow, fluid, bed, thickness, mask, density)
    copies = [pltpu.make_async_copy(a, b, arrived.at[i]) for i, (a, b) in enumerate(zip(far, near, strict=True))]
    for copy in copies:
        copy.start()
    for copy in copies:
        copy.wait()
    parts, levels, columns, _ = flow.shape
    upward = even("gx")
    height = thickness[...]
    flat = (bed[...] + height, height, mask[...].astype(jnp.float32))
    for part, level, width, place in side_planes(parts, levels):
        plane = flow.at[part, level] if part < parts else fluid.at[level] if part == parts else flat[level]
        low, high = plane[:width, :], plane[columns - width :, :]
        to_near[place : place + width, :] = jnp.where(upward, high, low)
        to_next[place : place + width, :] = jnp.where(upward, low, high)
    above = even("gz")
    for index, (part, number) in enumerate(face_planes(parts)):
        low, high = (start + number for start in face_starts(part, parts, levels))
        whole = flow.at[part] if part < parts else fluid
        spot = slice(index * columns, (index + 1) * columns)
        to_level[spot, :] = whole[jnp.where(above, low, high)]
    lead = MARGIN + WINDOW
    for part in range(parts + 1):
        for level in range(levels):
            plane = flow.at[part, level] if part < parts else fluid.at[level]
            state[part, level, lead : lead + columns, :] = plane[...]
    for number, plane in enumerate(flat):
        planes[number, lead : lead + columns, :] = plane
    weight[...] = jnp.sum(density[...], axis=0)


def unpaired(axis):
    place = lax.axis_index(axis)
    return (place == 0) | (place == lax.axis_size(axis) - 1)


def beside(near, next_, place, width, fluid_plane):
    inner = near[place : place + width, :]
    beyond = next_[place : place + width, :]
    if fluid_plane:
        beyond = jnp.where(unpaired("gx"), jnp.inf, beyond)
    return jnp.where(even("gx"), beyond, inner), jnp.where(even("gx"), inner, beyond)


def widen(state_in, planes_in, weight, next_, near, state, planes, to_next, to_near):
    parts, levels, tall, _ = state_in.shape
    parts -= 1
    rows = tall - 2 * MARGIN
    lead = MARGIN + WINDOW
    tail = MARGIN + rows - WINDOW
    upward = even("gz")
    for part, level, width, place in side_planes(parts, levels):
        before, after = beside(near, next_, place, width, part == parts)
        source, target = (state_in, state) if part <= parts else (planes_in, planes)
        spot = (part, level) if part <= parts else (level,)
        target[spot] = source[spot]
        target[(*spot, slice(lead - width, lead), slice(None))] = before
        target[(*spot, slice(tail, tail + width), slice(None))] = after
    count = 0
    for index, (part, number) in enumerate(face_planes(parts)):
        low, high = (start + number for start in face_starts(part, parts, levels))
        to_near[index * rows : (index + 1) * rows, :] = state[
            part, jnp.where(upward, high, low), MARGIN : MARGIN + rows, :
        ]
        level = jnp.where(upward, low, high)
        spot = 2 * WINDOW * index
        to_next[spot : spot + WINDOW, :] = state[part, level, MARGIN:lead, :]
        to_next[spot + WINDOW : spot + 2 * WINDOW, :] = state[part, level, tail : tail + WINDOW, :]
        count = index + 1
    to_near[count * rows :, :] = weight[...]


def along_y(field):
    lane = lax.broadcasted_iota(jnp.int32, field.shape, 1)
    end = field.shape[1] - 1
    upper = jnp.where(lane < end, pltpu.roll(field, end, 1), 0.0)
    lower = jnp.where(lane > 0, pltpu.roll(field, 1, 1), 0.0)
    return upper - lower


def window(rows):
    return tuple(slice(MARGIN + shift, MARGIN + shift + rows) for shift in (0, 1, -1))


def strain(rows, cells, k, stress, extra):
    win, ahead, behind = window(rows)

    def across(part):
        return cells(part, k)[ahead, :] - cells(part, k)[behind, :]

    def upward(part):
        return cells(part, k + 1)[win, :] - cells(part, k - 1)[win, :]

    def sideways(part):
        return along_y(cells(part, k)[win, :])

    xx = across(0)
    yy = sideways(1)
    zz = upward(2)
    xy = sideways(0) + across(1)
    xz = upward(0) + across(2)
    yz = upward(1) + sideways(2)
    second = 2.0 * (xx * xx + yy * yy + zz * zz) + (xy * xy + xz * xz + yz * yz)
    base = cells(4, k)[win, :] * (second * 0.0625 + REGULAR)
    root = jnp.exp2(jnp.log2(base) * (-1.0 / 3.0))
    pressure = cells(3, k)[win, :]
    push = 4.0 * pressure
    twice = 2.0 * root
    stress(0, k)[win, :] = twice * xx - push
    stress(1, k)[win, :] = twice * yy - push
    stress(2, k)[win, :] = twice * zz - push
    stress(3, k)[win, :] = root * xy
    stress(4, k)[win, :] = root * xz
    stress(5, k)[win, :] = root * yz
    extra(0, k)[...] = 0.05 * (base * (root * root))
    extra(1, k)[...] = pressure - (0.05 * root) * (xx + yy + zz)


def moved_on(rows, cells, stress, extra, k, slopes, ice, drag):
    win, ahead, behind = window(rows)

    def across(which):
        return stress(which, k)[ahead, :] - stress(which, k)[behind, :]

    def upward(which):
        return stress(which, k + 1)[win, :] - stress(which, k - 1)[win, :]

    def sideways(which):
        return along_y(stress(which, k)[win, :])

    factor = extra(0, k)[...]
    inside = ice[...] > 0.5
    u, v, w = (cells(part, k)[win, :] for part in range(3))
    force_x = across(0) + sideways(3) + upward(4) - slopes[0]
    force_y = across(3) + sideways(1) + upward(5) - slopes[1]
    force_z = across(4) + sideways(5) + upward(2)
    if drag is not None:
        force_x = force_x - drag[...] * u
        force_y = force_y - drag[...] * v
    return (
        jnp.where(inside, u + factor * force_x, 0.0),
        jnp.where(inside, v + factor * force_y, 0.0),
        jnp.where(inside, w + factor * force_z, 0.0),
        jnp.where(inside, extra(1, k)[...], 0.0),
    )


def shared(rows, planes, slopes, marks):
    win, ahead, behind = window(rows)
    lowest = lax.axis_index("gz") == 0
    highest = lax.axis_index("gz") == lax.axis_size("gz") - 1
    slopes[0] = 4.0 * (planes[0, ahead, :] - planes[0, behind, :])
    slopes[1] = 4.0 * along_y(planes[0, win, :])
    kind = planes[2, win, :]
    ice = jnp.where(kind > 0.5, 1.0, 0.0)
    marks[0] = jnp.where(lowest, 0.0, ice)
    marks[1] = ice
    marks[2] = jnp.where(highest, 0.0, ice)
    marks[3] = jnp.where(lowest & (kind > 0.5) & (kind < 1.5), 16.0, 0.0)


def inner(state, planes, stress, extra, fresh, slopes, marks):
    levels, tall, _ = state.shape[1:]
    rows = tall - 2 * MARGIN
    win, _, _ = window(rows)

    def cells(part, k):
        return state.at[part, k - DEEP]

    def stresses(which, k):
        return stress.at[which, k - DEEP - 1]

    def extras(which, k):
        return extra.at[which, k - DEEP - 1]

    shared(rows, planes, slopes, marks)
    for k in range(DEEP + 1, DEEP + levels - 1):
        strain(rows, cells, k, stresses, extras)
    for k in range(DEEP + 2, DEEP + levels - 2):
        for part, value in enumerate(moved_on(rows, cells, stresses, extras, k, slopes, marks.at[1], None)):
            fresh[part, k - DEEP - 2, win, :] = value


def evolve(
    own, planes, weight, stress_in, extra_in, fresh, face_next, edge_next, face_near,
    out, message, beyond, later, stress, extra, slopes, marks,
):
    parts, levels, columns, lanes = out.shape
    rows = columns + 2 * WINDOW
    deep = levels + 2 * DEEP
    win, _, _ = window(rows)
    upward = even("gz")
    lead = MARGIN + WINDOW
    tail = lead + columns

    count = 0
    for index, (part, number) in enumerate(face_planes(parts)):
        lower = 0 if part < parts - 1 else 1
        whole = face_near[rows * index : rows * (index + 1), :]
        beyond[part, number + jnp.where(upward, DEEP, lower), win, :] = whole
        middle = face_next[columns * index : columns * (index + 1), :]
        sides = edge_next[2 * WINDOW * index : 2 * WINDOW * (index + 1), :]
        if part == parts:
            middle, sides = (jnp.where(unpaired("gz"), jnp.inf, each) for each in (middle, sides))
        level = number + jnp.where(upward, lower, DEEP)
        beyond[part, level, lead - WINDOW : lead, :] = sides[:WINDOW, :]
        beyond[part, level, lead:tail, :] = middle
        beyond[part, level, tail : tail + WINDOW, :] = sides[WINDOW:, :]
        count = index + 1
    shared(rows, planes, slopes, marks)

    def before(part, k):
        if DEEP <= k < DEEP + levels:
            return own.at[part, k - DEEP]
        return beyond.at[part, k if k < DEEP else k - levels]

    def between(part, k):
        if part == parts:
            return before(part, k)
        if DEEP + 2 <= k < DEEP + levels - 2:
            return fresh.at[part, k - DEEP - 2]
        return later.at[part, k]

    def is_inner(k):
        return DEEP + 1 <= k < DEEP + levels - 1

    def stress_one(which, k):
        return stress_in.at[which, k - DEEP - 1] if is_inner(k) else stress.at[which, k]

    def extra_one(which, k):
        return extra_in.at[which, k - DEEP - 1] if is_inner(k) else extra.at[which, k]

    def stress_two(which, k):
        return stress.at[which, k]

    def extra_two(which, k):
        return extra.at[which, k]

    for k in range(1, deep - 1):
        if not is_inner(k):
            strain(rows, before, k, stress_one, extra_one)
    for k in range(2, deep - 2):
        if DEEP + 2 <= k < DEEP + levels - 2:
            continue
        ice = marks.at[0 if k < DEEP else 1 if k < DEEP + levels else 2]
        drag = marks.at[3] if k == DEEP else None
        for part, value in enumerate(moved_on(rows, before, stress_one, extra_one, k, slopes, ice, drag)):
            later[part, k, win, :] = value
    for k in range(3, deep - 3):
        strain(rows, between, k, stress_two, extra_two)
    cut = slice(WINDOW, WINDOW + columns)
    sum_u = sum_v = jnp.zeros((rows, lanes), jnp.float32)
    for k in range(DEEP, DEEP + levels):
        drag = marks.at[3] if k == DEEP else None
        values = moved_on(rows, between, stress_two, extra_two, k, slopes, marks.at[1], drag)
        for part, value in enumerate(values):
            out[part, k - DEEP] = value[cut, :]
        sum_u, sum_v = sum_u + values[0], sum_v + values[1]

    half = 0.5 / (levels * lax.axis_size("gz"))
    height = planes[1, win, :]
    slopes[0] = height * sum_u
    flux_y = along_y(height * sum_v)
    flux_x = slopes[0, WINDOW + 1 : WINDOW + columns + 1, :] - slopes[0, WINDOW - 1 : WINDOW + columns - 1, :]
    spread = half * (flux_x + flux_y[cut, :])
    both = weight[...] + face_near[count * rows :, :]
    part_of_both = jnp.where(upward, both[: columns // 2, :], both[columns // 2 :, :])
    for target in range(message.shape[0]):
        message[target, :columns, :] = spread
        message[target, columns:, :] = part_of_both


def finish(message, density, thickness, smb, other, moved, far_moved, far_grown, far_burden, grown, burden, sent):
    copies = [
        pltpu.make_async_copy(a, b, sent.at[i])
        for i, (a, b) in enumerate(((moved, far_moved), (grown, far_grown), (burden, far_burden)))
    ]
    copies[0].start()
    devices = message.shape[0]
    levels, columns, _ = density.shape
    count = other.shape[0] - columns
    place = lax.axis_index("gz")
    spread = message[0, :columns, :]
    for device in range(1, devices):
        spread = spread + message[device, :columns, :]
    over = jnp.where(even("gz"), other[count:, :], 0.0)
    for device in range(2, devices, 2):
        both = jnp.concatenate([message[device, columns:, :], message[device + 1, columns:, :]], axis=0)
        over = over + jnp.where(place < device, both, 0.0)
    new = thickness[...] + 0.5 * (smb[...] - spread)
    grown[...] = new
    copies[1].start()
    scaled = new * (1.0 / (levels * devices))
    for level in range(levels - 1, -1, -1):
        here = density[level]
        burden[level] = scaled * (over + 0.5 * here)
        over = over + here
    copies[2].start()
    for copy in copies:
        copy.wait()


def pairs_of(axis):
    near = [(i, i ^ 1) for i in range(lax.axis_size(axis))]
    return near, [(i + 1, j + 1) for i, j in near[:-2]]


def body(flow, fluid, density, thickness, bed, smb, mask):
    parts, levels, columns, lanes = flow.shape
    rows = columns + 2 * WINDOW
    deep = levels + 2 * DEEP
    tall = rows + 2 * MARGIN
    near_x, next_x = pairs_of("gx")
    near_z, next_z = pairs_of("gz")

    *_, (_, _, width, place) = side_planes(parts, levels)
    side = f32(place + width, lanes)
    faces = (parts + 1) * DEEP - 2
    wide = f32(parts + 1, levels, tall, lanes)
    flat = f32(3, tall, lanes)
    plane = f32(columns, lanes)
    inputs = (flow, fluid, bed, thickness, mask, density)
    to_near, to_next, to_level, state, planes, weight = call(
        prepare,
        (side, side, f32(faces * columns, lanes), wide, flat, plane),
        in_specs=[pl.BlockSpec(memory_space=pltpu.HBM)] * len(inputs),
        scratch=[pltpu.VMEM(each.shape, each.dtype) for each in inputs] + [pltpu.SemaphoreType.DMA((len(inputs),))],
    )(*(pltpu.with_memory_space_constraint(each, pltpu.HBM) for each in inputs))
    next_ = lax.ppermute(to_next, "gx", next_x)
    near = lax.ppermute(to_near, "gx", near_x)
    face_next = lax.ppermute(to_level, "gz", next_z)

    state, planes, to_next, to_near = call(
        widen, (wide, flat, f32(faces * 2 * WINDOW, lanes), f32(faces * rows + columns, lanes))
    )(state, planes, weight, next_, near)
    edge_next = lax.ppermute(to_next, "gz", next_z)
    face_near = lax.ppermute(to_near, "gz", near_z)

    stress, extra, fresh = call(
        inner,
        (f32(6, levels - 2, tall, lanes), f32(2, levels - 2, rows, lanes), f32(parts, levels - 4, tall, lanes)),
        scratch=[pltpu.VMEM((2, rows, lanes), jnp.float32), pltpu.VMEM((4, rows, lanes), jnp.float32)],
        cost_estimate=pl.CostEstimate(flops=INNER_COST, bytes_accessed=INNER_COST, transcendentals=0),
    )(state, planes)

    message = f32(lax.axis_size("gz"), columns + columns // 2, lanes)
    moved, message = call(
        evolve,
        (f32(*flow.shape), message),
        scratch=[
            pltpu.VMEM((parts + 1, 2 * DEEP, tall, lanes), jnp.float32),
            pltpu.VMEM((parts, deep, tall, lanes), jnp.float32),
            pltpu.VMEM((6, deep, tall, lanes), jnp.float32),
            pltpu.VMEM((2, deep, rows, lanes), jnp.float32),
            pltpu.VMEM((2, rows, lanes), jnp.float32),
            pltpu.VMEM((4, rows, lanes), jnp.float32),
        ],
    )(state, planes, weight, stress, extra, fresh, face_next, edge_next, face_near)
    message = lax.all_to_all(message, "gz", split_axis=0, concat_axis=0, tiled=True)
    deep_plane = f32(*density.shape)
    moved, grown, burden = call(
        finish,
        (f32(*flow.shape), plane, deep_plane),
        out_specs=[pl.BlockSpec(memory_space=pltpu.HBM)] * 3,
        scratch=[
            pltpu.VMEM(plane.shape, jnp.float32),
            pltpu.VMEM(deep_plane.shape, jnp.float32),
            pltpu.SemaphoreType.DMA((3,)),
        ],
    )(message, density, thickness, smb, face_near, moved)
    return moved, grown, burden


def solution(mesh):
    level_split = P("gz", "gx", None)
    flat = P("gx", None)
    return jax.shard_map(
        body,
        mesh=mesh,
        in_specs=(P(None, "gz", "gx", None), level_split, level_split, flat, flat, flat, flat),
        out_specs=(P(None, "gz", "gx", None), flat, level_split),
        check_vma=False,
    )
```

```python
import jax
import jax.numpy as jnp
from jax import lax
from jax.experimental import pallas as pl
from jax.experimental.pallas import tpu as pltpu
from jax.sharding import PartitionSpec as P

REGULAR = 0.01

DEEP = 4
WIDE = 5
WINDOW = 4
FLAT = (4, 1, 3)
MARGIN = 8
VMEM_LIMIT = 24 * 1024 * 1024
INNER_COST = 5_000_000_000


def call(kernel, outs, scratch=(), **specs):
    return pl.pallas_call(
        kernel,
        out_shape=outs,
        scratch_shapes=scratch,
        compiler_params=pltpu.CompilerParams(vmem_limit_bytes=VMEM_LIMIT),
        **specs,
    )


def f32(*shape):
    return jax.ShapeDtypeStruct(shape, jnp.float32)


def side_planes(parts, levels):
    place = 0
    for part in range(parts + 1):
        for level in range(levels):
            width = WIDE if part < parts - 1 else WINDOW
            yield part, level, width, place
            place += width
    for number, width in enumerate(FLAT):
        yield parts + 1, number, width, place
        place += width


def even(axis):
    return lax.rem(lax.axis_index(axis), 2) == 0


def face_planes(parts):
    for part in range(parts + 1):
        for far in range(1, DEEP + (part < parts - 1)):
            yield part, far, (WIDE if part < parts - 1 else WINDOW) - far


def prepare(
    flow_far, fluid_far, bed_far, thickness_far, mask_far, density_far,
    to_near, to_next, flow, fluid, bed, thickness, mask, density, arrived,
):
    far = (flow_far, fluid_far, bed_far, thickness_far, mask_far, density_far)
    near = (flow, fluid, bed, thickness, mask, density)
    copies = [pltpu.make_async_copy(a, b, arrived.at[i]) for i, (a, b) in enumerate(zip(far, near, strict=True))]
    for copy in copies:
        copy.start()
    for copy in copies:
        copy.wait()
    parts, levels, columns, _ = flow.shape
    upward = even("gx")
    height = thickness[...]
    flat = (bed[...] + height, height, mask[...].astype(jnp.float32))
    for part, level, width, place in side_planes(parts, levels):
        plane = flow.at[part, level] if part < parts else fluid.at[level] if part == parts else flat[level]
        low, high = plane[:width, :], plane[columns - width :, :]
        to_near[place : place + width, :] = jnp.where(upward, high, low)
        to_next[place : place + width, :] = jnp.where(upward, low, high)


def lay(flow, fluid, bed, thickness, mask, density, to_below, to_above, state, planes, weight):
    parts, levels, columns, _ = flow.shape
    for index, (part, far, _) in enumerate(face_planes(parts)):
        whole = flow.at[part] if part < parts else fluid
        spot = slice(index * columns, (index + 1) * columns)
        to_below[spot, :] = whole[far - 1]
        to_above[spot, :] = whole[levels - far]
    lead = MARGIN + WINDOW
    for part in range(parts + 1):
        for level in range(levels):
            plane = flow.at[part, level] if part < parts else fluid.at[level]
            state[part, level, lead : lead + columns, :] = plane[...]
    height = thickness[...]
    for number, plane in enumerate((bed[...] + height, height, mask[...].astype(jnp.float32))):
        planes[number, lead : lead + columns, :] = plane
    total = jnp.sum(density[...], axis=0)
    weight[...] = total
    for out in (to_below, to_above):
        out[out.shape[0] - columns :, :] = total


def unpaired(axis):
    place = lax.axis_index(axis)
    return (place == 0) | (place == lax.axis_size(axis) - 1)


def beside(near, next_, place, width, fluid_plane):
    inner = near[place : place + width, :]
    beyond = next_[place : place + width, :]
    if fluid_plane:
        beyond = jnp.where(unpaired("gx"), jnp.inf, beyond)
    return jnp.where(even("gx"), beyond, inner), jnp.where(even("gx"), inner, beyond)


def widen(state_in, planes_in, next_, near, state, planes, to_below, to_above):
    parts, levels, tall, _ = state_in.shape
    parts -= 1
    rows = tall - 2 * MARGIN
    lead = MARGIN + WINDOW
    tail = MARGIN + rows - WINDOW
    for part, level, width, place in side_planes(parts, levels):
        before, after = beside(near, next_, place, width, part == parts)
        source, target = (state_in, state) if part <= parts else (planes_in, planes)
        spot = (part, level) if part <= parts else (level,)
        target[spot] = source[spot]
        target[(*spot, slice(lead - width, lead), slice(None))] = before
        target[(*spot, slice(tail, tail + width), slice(None))] = after
    place = 0
    for part, far, width in face_planes(parts):
        for out, level in ((to_below, far - 1), (to_above, levels - far)):
            out[place : place + width, :] = state[part, level, lead - width : lead, :]
            out[place + width : place + 2 * width, :] = state[part, level, tail : tail + width, :]
        place += 2 * width


def along_y(field):
    lane = lax.broadcasted_iota(jnp.int32, field.shape, 1)
    end = field.shape[1] - 1
    upper = jnp.where(lane < end, pltpu.roll(field, end, 1), 0.0)
    lower = jnp.where(lane > 0, pltpu.roll(field, 1, 1), 0.0)
    return upper - lower


def window(rows):
    return tuple(slice(MARGIN + shift, MARGIN + shift + rows) for shift in (0, 1, -1))


def strain(rows, cells, k, stress, extra):
    win, ahead, behind = window(rows)

    def across(part):
        return cells(part, k)[ahead, :] - cells(part, k)[behind, :]

    def upward(part):
        return cells(part, k + 1)[win, :] - cells(part, k - 1)[win, :]

    def sideways(part):
        return along_y(cells(part, k)[win, :])

    xx = across(0)
    yy = sideways(1)
    zz = upward(2)
    xy = sideways(0) + across(1)
    xz = upward(0) + across(2)
    yz = upward(1) + sideways(2)
    second = 2.0 * (xx * xx + yy * yy + zz * zz) + (xy * xy + xz * xz + yz * yz)
    base = cells(4, k)[win, :] * (second * 0.0625 + REGULAR)
    root = jnp.exp2(jnp.log2(base) * (-1.0 / 3.0))
    pressure = cells(3, k)[win, :]
    push = 4.0 * pressure
    twice = 2.0 * root
    stress(0, k)[win, :] = twice * xx - push
    stress(1, k)[win, :] = twice * yy - push
    stress(2, k)[win, :] = twice * zz - push
    stress(3, k)[win, :] = root * xy
    stress(4, k)[win, :] = root * xz
    stress(5, k)[win, :] = root * yz
    extra(0, k)[...] = 0.05 * (base * (root * root))
    extra(1, k)[...] = pressure - (0.05 * root) * (xx + yy + zz)


def moved_on(rows, cells, stress, extra, k, slopes, ice, drag):
    win, ahead, behind = window(rows)

    def across(which):
        return stress(which, k)[ahead, :] - stress(which, k)[behind, :]

    def upward(which):
        return stress(which, k + 1)[win, :] - stress(which, k - 1)[win, :]

    def sideways(which):
        return along_y(stress(which, k)[win, :])

    factor = extra(0, k)[...]
    inside = ice[...] > 0.5
    u, v, w = (cells(part, k)[win, :] for part in range(3))
    force_x = across(0) + sideways(3) + upward(4) - slopes[0]
    force_y = across(3) + sideways(1) + upward(5) - slopes[1]
    force_z = across(4) + sideways(5) + upward(2)
    if drag is not None:
        force_x = force_x - drag[...] * u
        force_y = force_y - drag[...] * v
    return (
        jnp.where(inside, u + factor * force_x, 0.0),
        jnp.where(inside, v + factor * force_y, 0.0),
        jnp.where(inside, w + factor * force_z, 0.0),
        jnp.where(inside, extra(1, k)[...], 0.0),
    )


def shared(rows, planes, slopes, marks):
    win, ahead, behind = window(rows)
    lowest = lax.axis_index("gz") == 0
    highest = lax.axis_index("gz") == lax.axis_size("gz") - 1
    slopes[0] = 4.0 * (planes[0, ahead, :] - planes[0, behind, :])
    slopes[1] = 4.0 * along_y(planes[0, win, :])
    kind = planes[2, win, :]
    ice = jnp.where(kind > 0.5, 1.0, 0.0)
    marks[0] = jnp.where(lowest, 0.0, ice)
    marks[1] = ice
    marks[2] = jnp.where(highest, 0.0, ice)
    marks[3] = jnp.where(lowest & (kind > 0.5) & (kind < 1.5), 16.0, 0.0)


def inner(state, planes, stress, extra, fresh, slopes, marks):
    levels, tall, _ = state.shape[1:]
    rows = tall - 2 * MARGIN
    win, _, _ = window(rows)

    def cells(part, k):
        return state.at[part, k - DEEP]

    def stresses(which, k):
        return stress.at[which, k - DEEP - 1]

    def extras(which, k):
        return extra.at[which, k - DEEP - 1]

    shared(rows, planes, slopes, marks)
    for k in range(DEEP + 1, DEEP + levels - 1):
        strain(rows, cells, k, stresses, extras)
    for k in range(DEEP + 2, DEEP + levels - 2):
        for part, value in enumerate(moved_on(rows, cells, stresses, extras, k, slopes, marks.at[1], None)):
            fresh[part, k - DEEP - 2, win, :] = value


def evolve(
    own, planes, weight, stress_in, extra_in, fresh, edge_below, edge_above, face_below, face_above,
    out, message, beyond, later, stress, extra, slopes, marks,
):
    parts, levels, columns, lanes = out.shape
    rows = columns + 2 * WINDOW
    deep = levels + 2 * DEEP
    win, _, _ = window(rows)
    lead = MARGIN + WINDOW
    tail = lead + columns

    lowest = lax.axis_index("gz") == 0
    highest = lax.axis_index("gz") == lax.axis_size("gz") - 1
    faces = face_below.shape[0] - columns
    place = 0
    for index, (part, far, width) in enumerate(face_planes(parts)):
        for face, edge, level, outside in (
            (face_below, edge_below, DEEP - far, lowest),
            (face_above, edge_above, DEEP + far - 1, highest),
        ):
            middle = face[columns * index : columns * (index + 1), :]
            left = edge[place : place + width, :]
            right = edge[place + width : place + 2 * width, :]
            value = jnp.inf if part == parts else 0.0
            middle, left, right = (jnp.where(outside, value, each) for each in (middle, left, right))
            beyond[part, level, lead - width : lead, :] = left
            beyond[part, level, lead:tail, :] = middle
            beyond[part, level, tail : tail + width, :] = right
        place += 2 * width
    shared(rows, planes, slopes, marks)

    def before(part, k):
        if DEEP <= k < DEEP + levels:
            return own.at[part, k - DEEP]
        return beyond.at[part, k if k < DEEP else k - levels]

    def between(part, k):
        if part == parts:
            return before(part, k)
        if DEEP + 2 <= k < DEEP + levels - 2:
            return fresh.at[part, k - DEEP - 2]
        return later.at[part, k]

    def is_inner(k):
        return DEEP + 1 <= k < DEEP + levels - 1

    def stress_one(which, k):
        return stress_in.at[which, k - DEEP - 1] if is_inner(k) else stress.at[which, k]

    def extra_one(which, k):
        return extra_in.at[which, k - DEEP - 1] if is_inner(k) else extra.at[which, k]

    def stress_two(which, k):
        return stress.at[which, k]

    def extra_two(which, k):
        return extra.at[which, k]

    for k in range(1, deep - 1):
        if not is_inner(k):
            strain(rows, before, k, stress_one, extra_one)
    for k in range(2, deep - 2):
        if DEEP + 2 <= k < DEEP + levels - 2:
            continue
        ice = marks.at[0 if k < DEEP else 1 if k < DEEP + levels else 2]
        drag = marks.at[3] if k == DEEP else None
        for part, value in enumerate(moved_on(rows, before, stress_one, extra_one, k, slopes, ice, drag)):
            later[part, k, win, :] = value
    for k in range(3, deep - 3):
        strain(rows, between, k, stress_two, extra_two)
    cut = slice(WINDOW, WINDOW + columns)
    sum_u = sum_v = jnp.zeros((rows, lanes), jnp.float32)
    for k in range(DEEP, DEEP + levels):
        drag = marks.at[3] if k == DEEP else None
        values = moved_on(rows, between, stress_two, extra_two, k, slopes, marks.at[1], drag)
        for part, value in enumerate(values):
            out[part, k - DEEP] = value[cut, :]
        sum_u, sum_v = sum_u + values[0], sum_v + values[1]

    half = 0.5 / (levels * lax.axis_size("gz"))
    height = planes[1, win, :]
    slopes[0] = height * sum_u
    flux_y = along_y(height * sum_v)
    flux_x = slopes[0, WINDOW + 1 : WINDOW + columns + 1, :] - slopes[0, WINDOW - 1 : WINDOW + columns - 1, :]
    spread = half * (flux_x + flux_y[cut, :])
    first = even("gz")
    both = weight[...] + jnp.where(first, face_above[faces:, :], face_below[faces:, :])
    part_of_both = jnp.where(first, both[: columns // 2, :], both[columns // 2 :, :])
    for target in range(message.shape[0]):
        message[target, :columns, :] = spread
        message[target, columns:, :] = part_of_both


def finish(message, density, thickness, smb, face_above, moved, far_moved, far_grown, far_burden, grown, burden, sent):
    copies = [
        pltpu.make_async_copy(a, b, sent.at[i])
        for i, (a, b) in enumerate(((moved, far_moved), (grown, far_grown), (burden, far_burden)))
    ]
    copies[0].start()
    devices = message.shape[0]
    levels, columns, _ = density.shape
    count = face_above.shape[0] - columns
    place = lax.axis_index("gz")
    spread = message[0, :columns, :]
    for device in range(1, devices):
        spread = spread + message[device, :columns, :]
    over = jnp.where(even("gz"), face_above[count:, :], 0.0)
    for device in range(2, devices, 2):
        both = jnp.concatenate([message[device, columns:, :], message[device + 1, columns:, :]], axis=0)
        over = over + jnp.where(place < device, both, 0.0)
    new = thickness[...] + 0.5 * (smb[...] - spread)
    grown[...] = new
    copies[1].start()
    scaled = new * (1.0 / (levels * devices))
    for level in range(levels - 1, -1, -1):
        here = density[level]
        burden[level] = scaled * (over + 0.5 * here)
        over = over + here
    copies[2].start()
    for copy in copies:
        copy.wait()


def pairs_of(axis):
    near = [(i, i ^ 1) for i in range(lax.axis_size(axis))]
    return near, [(i + 1, j + 1) for i, j in near[:-2]]


def body(flow, fluid, density, thickness, bed, smb, mask):
    parts, levels, columns, lanes = flow.shape
    rows = columns + 2 * WINDOW
    deep = levels + 2 * DEEP
    tall = rows + 2 * MARGIN
    near_x, next_x = pairs_of("gx")
    count = lax.axis_size("gz")
    up = [(i, (i + 1) % count) for i in range(count)]
    down = [(j, i) for i, j in up]

    *_, (_, _, width, place) = side_planes(parts, levels)
    side = f32(place + width, lanes)
    faces = (parts + 1) * DEEP - 2
    corners = sum(2 * width for _, _, width in face_planes(parts))
    wide = f32(parts + 1, levels, tall, lanes)
    flat = f32(3, tall, lanes)
    plane = f32(columns, lanes)
    inputs = (flow, fluid, bed, thickness, mask, density)
    to_near, to_next, *inputs = call(
        prepare,
        (side, side, *(jax.ShapeDtypeStruct(each.shape, each.dtype) for each in inputs)),
        in_specs=[pl.BlockSpec(memory_space=pltpu.HBM)] * len(inputs),
        scratch=[pltpu.SemaphoreType.DMA((len(inputs),))],
    )(*(pltpu.with_memory_space_constraint(each, pltpu.HBM) for each in inputs))
    face = f32((faces + 1) * columns, lanes)
    to_below, to_above, state, planes, weight = call(lay, (face, face, wide, flat, plane))(*inputs)
    next_ = lax.ppermute(to_next, "gx", next_x)
    near = lax.ppermute(to_near, "gx", near_x)
    face_below = lax.ppermute(to_above, "gz", up)
    face_above = lax.ppermute(to_below, "gz", down)

    edge = f32(corners, lanes)
    state, planes, to_below, to_above = call(widen, (wide, flat, edge, edge))(state, planes, next_, near)
    edge_below = lax.ppermute(to_above, "gz", up)
    edge_above = lax.ppermute(to_below, "gz", down)

    stress, extra, fresh = call(
        inner,
        (f32(6, levels - 2, tall, lanes), f32(2, levels - 2, rows, lanes), f32(parts, levels - 4, tall, lanes)),
        scratch=[pltpu.VMEM((2, rows, lanes), jnp.float32), pltpu.VMEM((4, rows, lanes), jnp.float32)],
        cost_estimate=pl.CostEstimate(flops=INNER_COST, bytes_accessed=INNER_COST, transcendentals=0),
    )(state, planes)

    message = f32(lax.axis_size("gz"), columns + columns // 2, lanes)
    moved, message = call(
        evolve,
        (f32(*flow.shape), message),
        scratch=[
            pltpu.VMEM((parts + 1, 2 * DEEP, tall, lanes), jnp.float32),
            pltpu.VMEM((parts, deep, tall, lanes), jnp.float32),
            pltpu.VMEM((6, deep, tall, lanes), jnp.float32),
            pltpu.VMEM((2, deep, rows, lanes), jnp.float32),
            pltpu.VMEM((2, rows, lanes), jnp.float32),
            pltpu.VMEM((4, rows, lanes), jnp.float32),
        ],
    )(state, planes, weight, stress, extra, fresh, edge_below, edge_above, face_below, face_above)
    message = lax.all_to_all(message, "gz", split_axis=0, concat_axis=0, tiled=True)
    deep_plane = f32(*density.shape)
    moved, grown, burden = call(
        finish,
        (f32(*flow.shape), plane, deep_plane),
        out_specs=[pl.BlockSpec(memory_space=pltpu.HBM)] * 3,
        scratch=[
            pltpu.VMEM(plane.shape, jnp.float32),
            pltpu.VMEM(deep_plane.shape, jnp.float32),
            pltpu.SemaphoreType.DMA((3,)),
        ],
    )(message, density, thickness, smb, face_above, moved)
    return moved, grown, burden


def solution(mesh):
    level_split = P("gz", "gx", None)
    flat = P("gx", None)
    return jax.shard_map(
        body,
        mesh=mesh,
        in_specs=(P(None, "gz", "gx", None), level_split, level_split, flat, flat, flat, flat),
        out_specs=(P(None, "gz", "gx", None), flat, level_split),
        check_vma=False,
    )
```

```python
import jax
import jax.numpy as jnp
from jax import lax
from jax.experimental import pallas as pl
from jax.experimental.pallas import tpu as pltpu
from jax.sharding import PartitionSpec as P

REGULAR = 0.01

DEEP = 4
WIDE = 5
WINDOW = 4
FLAT = (4, 1, 3)
MARGIN = 8
VMEM_LIMIT = 24 * 1024 * 1024
INNER_COST = 5_000_000_000


def call(kernel, outs, scratch=(), **specs):
    return pl.pallas_call(
        kernel,
        out_shape=outs,
        scratch_shapes=scratch,
        compiler_params=pltpu.CompilerParams(vmem_limit_bytes=VMEM_LIMIT),
        **specs,
    )


def f32(*shape):
    return jax.ShapeDtypeStruct(shape, jnp.float32)


def side_planes(parts, levels):
    place = 0
    for part in range(parts + 1):
        for level in range(levels):
            width = WIDE if part < parts - 1 else WINDOW
            yield part, level, width, place
            place += width
    for number, width in enumerate(FLAT):
        yield parts + 1, number, width, place
        place += width


def even(axis):
    return lax.rem(lax.axis_index(axis), 2) == 0


def face_planes(parts):
    for part in range(parts + 1):
        for far in range(1, DEEP + (part < parts - 1)):
            yield part, far, (WIDE if part < parts - 1 else WINDOW) - far


def prepare(
    flow_far, fluid_far, bed_far, thickness_far, mask_far, density_far,
    to_near, to_next, flow, fluid, bed, thickness, mask, density, arrived,
):
    far = (flow_far, fluid_far, bed_far, thickness_far, mask_far, density_far)
    near = (flow, fluid, bed, thickness, mask, density)
    copies = [pltpu.make_async_copy(a, b, arrived.at[i]) for i, (a, b) in enumerate(zip(far, near, strict=True))]
    for copy in copies:
        copy.start()
    for copy in copies:
        copy.wait()
    parts, levels, columns, _ = flow.shape
    upward = even("gx")
    height = thickness[...]
    flat = (bed[...] + height, height, mask[...].astype(jnp.float32))
    for part, level, width, place in side_planes(parts, levels):
        plane = flow.at[part, level] if part < parts else fluid.at[level] if part == parts else flat[level]
        low, high = plane[:width, :], plane[columns - width :, :]
        to_near[place : place + width, :] = jnp.where(upward, high, low)
        to_next[place : place + width, :] = jnp.where(upward, low, high)


def lay(flow, fluid, bed, thickness, mask, density, to_below, to_above, state, planes, weight):
    parts, levels, columns, _ = flow.shape
    for index, (part, far, _) in enumerate(face_planes(parts)):
        whole = flow.at[part] if part < parts else fluid
        spot = slice(index * columns, (index + 1) * columns)
        to_below[spot, :] = whole[far - 1]
        to_above[spot, :] = whole[levels - far]
    lead = MARGIN + WINDOW
    for part in range(parts + 1):
        for level in range(levels):
            plane = flow.at[part, level] if part < parts else fluid.at[level]
            state[part, level, lead : lead + columns, :] = plane[...]
    height = thickness[...]
    for number, plane in enumerate((bed[...] + height, height, mask[...].astype(jnp.float32))):
        planes[number, lead : lead + columns, :] = plane
    total = jnp.sum(density[...], axis=0)
    weight[...] = total
    for out in (to_below, to_above):
        out[out.shape[0] - columns :, :] = total


def unpaired(axis):
    place = lax.axis_index(axis)
    return (place == 0) | (place == lax.axis_size(axis) - 1)


def beside(near, next_, place, width, fluid_plane):
    inner = near[place : place + width, :]
    beyond = next_[place : place + width, :]
    if fluid_plane:
        beyond = jnp.where(unpaired("gx"), jnp.inf, beyond)
    return jnp.where(even("gx"), beyond, inner), jnp.where(even("gx"), inner, beyond)


def widen(state_in, planes_in, next_, near, state, planes, to_below, to_above):
    parts, levels, tall, _ = state_in.shape
    parts -= 1
    rows = tall - 2 * MARGIN
    lead = MARGIN + WINDOW
    tail = MARGIN + rows - WINDOW
    for part, level, width, place in side_planes(parts, levels):
        before, after = beside(near, next_, place, width, part == parts)
        source, target = (state_in, state) if part <= parts else (planes_in, planes)
        spot = (part, level) if part <= parts else (level,)
        target[spot] = source[spot]
        target[(*spot, slice(lead - width, lead), slice(None))] = before
        target[(*spot, slice(tail, tail + width), slice(None))] = after
    place = 0
    for part, far, width in face_planes(parts):
        for out, level in ((to_below, far - 1), (to_above, levels - far)):
            out[place : place + width, :] = state[part, level, lead - width : lead, :]
            out[place + width : place + 2 * width, :] = state[part, level, tail : tail + width, :]
        place += 2 * width


def along_y(field):
    lane = lax.broadcasted_iota(jnp.int32, field.shape, 1)
    end = field.shape[1] - 1
    upper = jnp.where(lane < end, pltpu.roll(field, end, 1), 0.0)
    lower = jnp.where(lane > 0, pltpu.roll(field, 1, 1), 0.0)
    return upper - lower


def window(rows):
    return tuple(slice(MARGIN + shift, MARGIN + shift + rows) for shift in (0, 1, -1))


def strain(rows, cells, k, stress, extra):
    win, ahead, behind = window(rows)

    def across(part):
        return cells(part, k)[ahead, :] - cells(part, k)[behind, :]

    def upward(part):
        return cells(part, k + 1)[win, :] - cells(part, k - 1)[win, :]

    def sideways(part):
        return along_y(cells(part, k)[win, :])

    xx = across(0)
    yy = sideways(1)
    zz = upward(2)
    xy = sideways(0) + across(1)
    xz = upward(0) + across(2)
    yz = upward(1) + sideways(2)
    second = 2.0 * (xx * xx + yy * yy + zz * zz) + (xy * xy + xz * xz + yz * yz)
    base = cells(4, k)[win, :] * (second * 0.0625 + REGULAR)
    root = jnp.exp2(jnp.log2(base) * (-1.0 / 3.0))
    pressure = cells(3, k)[win, :]
    push = 4.0 * pressure
    twice = 2.0 * root
    stress(0, k)[win, :] = twice * xx - push
    stress(1, k)[win, :] = twice * yy - push
    stress(2, k)[win, :] = twice * zz - push
    stress(3, k)[win, :] = root * xy
    stress(4, k)[win, :] = root * xz
    stress(5, k)[win, :] = root * yz
    extra(0, k)[...] = 0.05 * (base * (root * root))
    extra(1, k)[...] = pressure - (0.05 * root) * (xx + yy + zz)


def moved_on(rows, cells, stress, extra, k, slopes, ice, drag):
    win, ahead, behind = window(rows)

    def across(which):
        return stress(which, k)[ahead, :] - stress(which, k)[behind, :]

    def upward(which):
        return stress(which, k + 1)[win, :] - stress(which, k - 1)[win, :]

    def sideways(which):
        return along_y(stress(which, k)[win, :])

    factor = extra(0, k)[...]
    inside = ice[...] > 0.5
    u, v, w = (cells(part, k)[win, :] for part in range(3))
    force_x = across(0) + sideways(3) + upward(4) - slopes[0]
    force_y = across(3) + sideways(1) + upward(5) - slopes[1]
    force_z = across(4) + sideways(5) + upward(2)
    if drag is not None:
        force_x = force_x - drag[...] * u
        force_y = force_y - drag[...] * v
    return (
        jnp.where(inside, u + factor * force_x, 0.0),
        jnp.where(inside, v + factor * force_y, 0.0),
        jnp.where(inside, w + factor * force_z, 0.0),
        jnp.where(inside, extra(1, k)[...], 0.0),
    )


def shared(rows, planes, slopes, marks):
    win, ahead, behind = window(rows)
    lowest = lax.axis_index("gz") == 0
    highest = lax.axis_index("gz") == lax.axis_size("gz") - 1
    slopes[0] = 4.0 * (planes[0, ahead, :] - planes[0, behind, :])
    slopes[1] = 4.0 * along_y(planes[0, win, :])
    kind = planes[2, win, :]
    ice = jnp.where(kind > 0.5, 1.0, 0.0)
    marks[0] = jnp.where(lowest, 0.0, ice)
    marks[1] = ice
    marks[2] = jnp.where(highest, 0.0, ice)
    marks[3] = jnp.where(lowest & (kind > 0.5) & (kind < 1.5), 16.0, 0.0)


def inner(state, planes, stress, extra, fresh, slopes, marks):
    levels, tall, _ = state.shape[1:]
    rows = tall - 2 * MARGIN
    win, _, _ = window(rows)

    def cells(part, k):
        return state.at[part, k - DEEP]

    def stresses(which, k):
        return stress.at[which, k - DEEP - 1]

    def extras(which, k):
        return extra.at[which, k - DEEP - 1]

    shared(rows, planes, slopes, marks)
    for k in range(DEEP + 1, DEEP + levels - 1):
        strain(rows, cells, k, stresses, extras)
    for k in range(DEEP + 2, DEEP + levels - 2):
        for part, value in enumerate(moved_on(rows, cells, stresses, extras, k, slopes, marks.at[1], None)):
            fresh[part, k - DEEP - 2, win, :] = value


def evolve(
    own, planes, weight, stress_in, extra_in, fresh, edge_above, edge_below, face_above, face_below,
    out, message, beyond, later, stress, extra, slopes, marks,
):
    parts, levels, columns, lanes = out.shape
    rows = columns + 2 * WINDOW
    deep = levels + 2 * DEEP
    win, _, _ = window(rows)
    lead = MARGIN + WINDOW
    tail = lead + columns

    lowest = lax.axis_index("gz") == 0
    highest = lax.axis_index("gz") == lax.axis_size("gz") - 1
    faces = face_below.shape[0] - columns
    place = 0
    for index, (part, far, width) in enumerate(face_planes(parts)):
        for face, edge, level, outside in (
            (face_below, edge_below, DEEP - far, lowest),
            (face_above, edge_above, DEEP + far - 1, highest),
        ):
            middle = face[columns * index : columns * (index + 1), :]
            left = edge[place : place + width, :]
            right = edge[place + width : place + 2 * width, :]
            value = jnp.inf if part == parts else 0.0
            middle, left, right = (jnp.where(outside, value, each) for each in (middle, left, right))
            beyond[part, level, lead - width : lead, :] = left
            beyond[part, level, lead:tail, :] = middle
            beyond[part, level, tail : tail + width, :] = right
        place += 2 * width
    shared(rows, planes, slopes, marks)

    def before(part, k):
        if DEEP <= k < DEEP + levels:
            return own.at[part, k - DEEP]
        return beyond.at[part, k if k < DEEP else k - levels]

    def between(part, k):
        if part == parts:
            return before(part, k)
        if DEEP + 2 <= k < DEEP + levels - 2:
            return fresh.at[part, k - DEEP - 2]
        return later.at[part, k]

    def is_inner(k):
        return DEEP + 1 <= k < DEEP + levels - 1

    def stress_one(which, k):
        return stress_in.at[which, k - DEEP - 1] if is_inner(k) else stress.at[which, k]

    def extra_one(which, k):
        return extra_in.at[which, k - DEEP - 1] if is_inner(k) else extra.at[which, k]

    def stress_two(which, k):
        return stress.at[which, k]

    def extra_two(which, k):
        return extra.at[which, k]

    for k in range(1, deep - 1):
        if not is_inner(k):
            strain(rows, before, k, stress_one, extra_one)
    for k in range(2, deep - 2):
        if DEEP + 2 <= k < DEEP + levels - 2:
            continue
        ice = marks.at[0 if k < DEEP else 1 if k < DEEP + levels else 2]
        drag = marks.at[3] if k == DEEP else None
        for part, value in enumerate(moved_on(rows, before, stress_one, extra_one, k, slopes, ice, drag)):
            later[part, k, win, :] = value
    for k in range(3, deep - 3):
        strain(rows, between, k, stress_two, extra_two)
    cut = slice(WINDOW, WINDOW + columns)
    sum_u = sum_v = jnp.zeros((rows, lanes), jnp.float32)
    for k in range(DEEP, DEEP + levels):
        drag = marks.at[3] if k == DEEP else None
        values = moved_on(rows, between, stress_two, extra_two, k, slopes, marks.at[1], drag)
        for part, value in enumerate(values):
            out[part, k - DEEP] = value[cut, :]
        sum_u, sum_v = sum_u + values[0], sum_v + values[1]

    half = 0.5 / (levels * lax.axis_size("gz"))
    height = planes[1, win, :]
    slopes[0] = height * sum_u
    flux_y = along_y(height * sum_v)
    flux_x = slopes[0, WINDOW + 1 : WINDOW + columns + 1, :] - slopes[0, WINDOW - 1 : WINDOW + columns - 1, :]
    spread = half * (flux_x + flux_y[cut, :])
    first = even("gz")
    both = weight[...] + jnp.where(first, face_above[faces:, :], face_below[faces:, :])
    part_of_both = jnp.where(first, both[: columns // 2, :], both[columns // 2 :, :])
    for target in range(message.shape[0]):
        message[target, :columns, :] = spread
        message[target, columns:, :] = part_of_both


def finish(message, density, thickness, smb, face_above, moved, far_moved, far_grown, far_burden, grown, burden, sent):
    copies = [
        pltpu.make_async_copy(a, b, sent.at[i])
        for i, (a, b) in enumerate(((moved, far_moved), (grown, far_grown), (burden, far_burden)))
    ]
    copies[0].start()
    devices = message.shape[0]
    levels, columns, _ = density.shape
    count = face_above.shape[0] - columns
    place = lax.axis_index("gz")
    spread = message[0, :columns, :]
    for device in range(1, devices):
        spread = spread + message[device, :columns, :]
    over = jnp.where(even("gz"), face_above[count:, :], 0.0)
    for device in range(2, devices, 2):
        both = jnp.concatenate([message[device, columns:, :], message[device + 1, columns:, :]], axis=0)
        over = over + jnp.where(place < device, both, 0.0)
    new = thickness[...] + 0.5 * (smb[...] - spread)
    grown[...] = new
    copies[1].start()
    scaled = new * (1.0 / (levels * devices))
    for level in range(levels - 1, -1, -1):
        here = density[level]
        burden[level] = scaled * (over + 0.5 * here)
        over = over + here
    copies[2].start()
    for copy in copies:
        copy.wait()


def pairs_of(axis):
    near = [(i, i ^ 1) for i in range(lax.axis_size(axis))]
    return near, [(i + 1, j + 1) for i, j in near[:-2]]


def body(flow, fluid, density, thickness, bed, smb, mask):
    parts, levels, columns, lanes = flow.shape
    rows = columns + 2 * WINDOW
    deep = levels + 2 * DEEP
    tall = rows + 2 * MARGIN
    near_x, next_x = pairs_of("gx")
    count = lax.axis_size("gz")
    up = [(i, (i + 1) % count) for i in range(count)]
    down = [(j, i) for i, j in up]

    *_, (_, _, width, place) = side_planes(parts, levels)
    side = f32(place + width, lanes)
    faces = (parts + 1) * DEEP - 2
    corners = sum(2 * width for _, _, width in face_planes(parts))
    wide = f32(parts + 1, levels, tall, lanes)
    flat = f32(3, tall, lanes)
    plane = f32(columns, lanes)
    inputs = (flow, fluid, bed, thickness, mask, density)
    to_near, to_next, *inputs = call(
        prepare,
        (side, side, *(jax.ShapeDtypeStruct(each.shape, each.dtype) for each in inputs)),
        in_specs=[pl.BlockSpec(memory_space=pltpu.HBM)] * len(inputs),
        scratch=[pltpu.SemaphoreType.DMA((len(inputs),))],
    )(*(pltpu.with_memory_space_constraint(each, pltpu.HBM) for each in inputs))
    face = f32((faces + 1) * columns, lanes)
    to_below, to_above, state, planes, weight = call(lay, (face, face, wide, flat, plane))(*inputs)
    next_ = lax.ppermute(to_next, "gx", next_x)
    near = lax.ppermute(to_near, "gx", near_x)
    face_below = lax.ppermute(to_above, "gz", up)
    face_above = lax.ppermute(to_below, "gz", down)

    edge = f32(corners, lanes)
    state, planes, to_below, to_above = call(widen, (wide, flat, edge, edge))(state, planes, next_, near)
    edge_below = lax.ppermute(to_above, "gz", up)
    edge_above = lax.ppermute(to_below, "gz", down)

    stress, extra, fresh = call(
        inner,
        (f32(6, levels - 2, tall, lanes), f32(2, levels - 2, rows, lanes), f32(parts, levels - 4, tall, lanes)),
        scratch=[pltpu.VMEM((2, rows, lanes), jnp.float32), pltpu.VMEM((4, rows, lanes), jnp.float32)],
        cost_estimate=pl.CostEstimate(flops=INNER_COST, bytes_accessed=INNER_COST, transcendentals=0),
    )(state, planes)

    message = f32(lax.axis_size("gz"), columns + columns // 2, lanes)
    moved, message = call(
        evolve,
        (f32(*flow.shape), message),
        scratch=[
            pltpu.VMEM((parts + 1, 2 * DEEP, tall, lanes), jnp.float32),
            pltpu.VMEM((parts, deep, tall, lanes), jnp.float32),
            pltpu.VMEM((6, deep, tall, lanes), jnp.float32),
            pltpu.VMEM((2, deep, rows, lanes), jnp.float32),
            pltpu.VMEM((2, rows, lanes), jnp.float32),
            pltpu.VMEM((4, rows, lanes), jnp.float32),
        ],
    )(state, planes, weight, stress, extra, fresh, edge_above, edge_below, face_above, face_below)
    message = lax.all_to_all(message, "gz", split_axis=0, concat_axis=0, tiled=True)
    deep_plane = f32(*density.shape)
    moved, grown, burden = call(
        finish,
        (f32(*flow.shape), plane, deep_plane),
        out_specs=[pl.BlockSpec(memory_space=pltpu.HBM)] * 3,
        scratch=[
            pltpu.VMEM(plane.shape, jnp.float32),
            pltpu.VMEM(deep_plane.shape, jnp.float32),
            pltpu.SemaphoreType.DMA((3,)),
        ],
    )(message, density, thickness, smb, face_above, moved)
    return moved, grown, burden


def solution(mesh):
    level_split = P("gz", "gx", None)
    flat = P("gx", None)
    return jax.shard_map(
        body,
        mesh=mesh,
        in_specs=(P(None, "gz", "gx", None), level_split, level_split, flat, flat, flat, flat),
        out_specs=(P(None, "gz", "gx", None), flat, level_split),
        check_vma=False,
    )
```

```python
import jax
import jax.numpy as jnp
from jax import lax
from jax.experimental import pallas as pl
from jax.experimental.pallas import tpu as pltpu
from jax.sharding import PartitionSpec as P

REGULAR = 0.01

DEEP = 4
WIDE = 5
WINDOW = 4
FLAT = (4, 1, 3)
MARGIN = 8
VMEM_LIMIT = 24 * 1024 * 1024
INNER_COST = 5_000_000_000


def call(kernel, outs, scratch=(), **specs):
    return pl.pallas_call(
        kernel,
        out_shape=outs,
        scratch_shapes=scratch,
        compiler_params=pltpu.CompilerParams(vmem_limit_bytes=VMEM_LIMIT),
        **specs,
    )


def f32(*shape):
    return jax.ShapeDtypeStruct(shape, jnp.float32)


def side_planes(parts, levels):
    place = 0
    for part in range(parts + 1):
        for level in range(levels):
            width = WIDE if part < parts - 1 else WINDOW
            yield part, level, width, place
            place += width
    for number, width in enumerate(FLAT):
        yield parts + 1, number, width, place
        place += width


def even(axis):
    return lax.rem(lax.axis_index(axis), 2) == 0


def face_planes(parts):
    for part in range(parts + 1):
        for far in range(1, DEEP + (part < parts - 1)):
            yield part, far, (WIDE if part < parts - 1 else WINDOW) - far


def prepare(
    flow_far, fluid_far, bed_far, thickness_far, mask_far, density_far,
    to_near, to_next, flow, fluid, bed, thickness, mask, density, arrived,
):
    far = (flow_far, fluid_far, bed_far, thickness_far, mask_far, density_far)
    near = (flow, fluid, bed, thickness, mask, density)
    copies = [pltpu.make_async_copy(a, b, arrived.at[i]) for i, (a, b) in enumerate(zip(far, near, strict=True))]
    for copy in copies:
        copy.start()
    for copy in copies:
        copy.wait()
    parts, levels, columns, _ = flow.shape
    upward = even("gx")
    height = thickness[...]
    flat = (bed[...] + height, height, mask[...].astype(jnp.float32))
    for part, level, width, place in side_planes(parts, levels):
        plane = flow.at[part, level] if part < parts else fluid.at[level] if part == parts else flat[level]
        low, high = plane[:width, :], plane[columns - width :, :]
        to_near[place : place + width, :] = jnp.where(upward, high, low)
        to_next[place : place + width, :] = jnp.where(upward, low, high)


def lay(flow, fluid, bed, thickness, mask, density, to_below, to_above, state, planes, weight):
    parts, levels, columns, _ = flow.shape
    for index, (part, far, _) in enumerate(face_planes(parts)):
        whole = flow.at[part] if part < parts else fluid
        spot = slice(index * columns, (index + 1) * columns)
        to_below[spot, :] = whole[far - 1]
        to_above[spot, :] = whole[levels - far]
    lead = MARGIN + WINDOW
    for part in range(parts + 1):
        for level in range(levels):
            plane = flow.at[part, level] if part < parts else fluid.at[level]
            state[part, level, lead : lead + columns, :] = plane[...]
    height = thickness[...]
    for number, plane in enumerate((bed[...] + height, height, mask[...].astype(jnp.float32))):
        planes[number, lead : lead + columns, :] = plane
    total = jnp.sum(density[...], axis=0)
    weight[...] = total
    for out in (to_below, to_above):
        out[out.shape[0] - columns :, :] = total


def unpaired(axis):
    place = lax.axis_index(axis)
    return (place == 0) | (place == lax.axis_size(axis) - 1)


def beside(near, next_, place, width, fluid_plane):
    inner = near[place : place + width, :]
    beyond = next_[place : place + width, :]
    if fluid_plane:
        beyond = jnp.where(unpaired("gx"), jnp.inf, beyond)
    return jnp.where(even("gx"), beyond, inner), jnp.where(even("gx"), inner, beyond)


def widen(state_in, planes_in, next_, near, state, planes, to_below, to_above):
    parts, levels, tall, _ = state_in.shape
    parts -= 1
    rows = tall - 2 * MARGIN
    lead = MARGIN + WINDOW
    tail = MARGIN + rows - WINDOW
    for part, level, width, place in side_planes(parts, levels):
        before, after = beside(near, next_, place, width, part == parts)
        source, target = (state_in, state) if part <= parts else (planes_in, planes)
        spot = (part, level) if part <= parts else (level,)
        target[spot] = source[spot]
        target[(*spot, slice(lead - width, lead), slice(None))] = before
        target[(*spot, slice(tail, tail + width), slice(None))] = after
    place = 0
    for part, far, width in face_planes(parts):
        for out, level in ((to_below, far - 1), (to_above, levels - far)):
            out[place : place + width, :] = state[part, level, lead - width : lead, :]
            out[place + width : place + 2 * width, :] = state[part, level, tail : tail + width, :]
        place += 2 * width


def along_y(field):
    lane = lax.broadcasted_iota(jnp.int32, field.shape, 1)
    end = field.shape[1] - 1
    upper = jnp.where(lane < end, pltpu.roll(field, end, 1), 0.0)
    lower = jnp.where(lane > 0, pltpu.roll(field, 1, 1), 0.0)
    return upper - lower


def window(rows):
    return tuple(slice(MARGIN + shift, MARGIN + shift + rows) for shift in (0, 1, -1))


def strain(rows, cells, k, stress, extra):
    win, ahead, behind = window(rows)

    def across(part):
        return cells(part, k)[ahead, :] - cells(part, k)[behind, :]

    def upward(part):
        return cells(part, k + 1)[win, :] - cells(part, k - 1)[win, :]

    def sideways(part):
        return along_y(cells(part, k)[win, :])

    xx = across(0)
    yy = sideways(1)
    zz = upward(2)
    xy = sideways(0) + across(1)
    xz = upward(0) + across(2)
    yz = upward(1) + sideways(2)
    second = 2.0 * (xx * xx + yy * yy + zz * zz) + (xy * xy + xz * xz + yz * yz)
    base = cells(4, k)[win, :] * (second * 0.0625 + REGULAR)
    root = jnp.exp2(jnp.log2(base) * (-1.0 / 3.0))
    pressure = cells(3, k)[win, :]
    push = 4.0 * pressure
    twice = 2.0 * root
    stress(0, k)[win, :] = twice * xx - push
    stress(1, k)[win, :] = twice * yy - push
    stress(2, k)[win, :] = twice * zz - push
    stress(3, k)[win, :] = root * xy
    stress(4, k)[win, :] = root * xz
    stress(5, k)[win, :] = root * yz
    extra(0, k)[...] = 0.05 * (base * (root * root))
    extra(1, k)[...] = pressure - (0.05 * root) * (xx + yy + zz)


def moved_on(rows, cells, stress, extra, k, slopes, ice, drag):
    win, ahead, behind = window(rows)

    def across(which):
        return stress(which, k)[ahead, :] - stress(which, k)[behind, :]

    def upward(which):
        return stress(which, k + 1)[win, :] - stress(which, k - 1)[win, :]

    def sideways(which):
        return along_y(stress(which, k)[win, :])

    factor = extra(0, k)[...]
    inside = ice[...] > 0.5
    u, v, w = (cells(part, k)[win, :] for part in range(3))
    force_x = across(0) + sideways(3) + upward(4) - slopes[0]
    force_y = across(3) + sideways(1) + upward(5) - slopes[1]
    force_z = across(4) + sideways(5) + upward(2)
    if drag is not None:
        force_x = force_x - drag[...] * u
        force_y = force_y - drag[...] * v
    return (
        jnp.where(inside, u + factor * force_x, 0.0),
        jnp.where(inside, v + factor * force_y, 0.0),
        jnp.where(inside, w + factor * force_z, 0.0),
        jnp.where(inside, extra(1, k)[...], 0.0),
    )


def shared(rows, planes, slopes, marks):
    win, ahead, behind = window(rows)
    lowest = lax.axis_index("gz") == 0
    highest = lax.axis_index("gz") == lax.axis_size("gz") - 1
    slopes[0] = 4.0 * (planes[0, ahead, :] - planes[0, behind, :])
    slopes[1] = 4.0 * along_y(planes[0, win, :])
    kind = planes[2, win, :]
    ice = jnp.where(kind > 0.5, 1.0, 0.0)
    marks[0] = jnp.where(lowest, 0.0, ice)
    marks[1] = ice
    marks[2] = jnp.where(highest, 0.0, ice)
    marks[3] = jnp.where(lowest & (kind > 0.5) & (kind < 1.5), 16.0, 0.0)


def inner(state, planes, stress, extra, fresh, slopes, marks):
    levels, tall, _ = state.shape[1:]
    rows = tall - 2 * MARGIN
    win, _, _ = window(rows)

    def cells(part, k):
        return state.at[part, k - DEEP]

    def stresses(which, k):
        return stress.at[which, k - DEEP - 1]

    def extras(which, k):
        return extra.at[which, k - DEEP - 1]

    shared(rows, planes, slopes, marks)
    for k in range(DEEP + 1, DEEP + levels - 1):
        strain(rows, cells, k, stresses, extras)
    for k in range(DEEP + 2, DEEP + levels - 2):
        for part, value in enumerate(moved_on(rows, cells, stresses, extras, k, slopes, marks.at[1], None)):
            fresh[part, k - DEEP - 2, win, :] = value


def evolve(
    own, planes, weight, stress_in, extra_in, fresh, edge_below, edge_above, face_above, face_below,
    out, message, beyond, later, stress, extra, slopes, marks,
):
    parts, levels, columns, lanes = out.shape
    rows = columns + 2 * WINDOW
    deep = levels + 2 * DEEP
    win, _, _ = window(rows)
    lead = MARGIN + WINDOW
    tail = lead + columns

    lowest = lax.axis_index("gz") == 0
    highest = lax.axis_index("gz") == lax.axis_size("gz") - 1
    faces = face_below.shape[0] - columns
    place = 0
    for index, (part, far, width) in enumerate(face_planes(parts)):
        for face, edge, level, outside in (
            (face_below, edge_below, DEEP - far, lowest),
            (face_above, edge_above, DEEP + far - 1, highest),
        ):
            middle = face[columns * index : columns * (index + 1), :]
            left = edge[place : place + width, :]
            right = edge[place + width : place + 2 * width, :]
            value = jnp.inf if part == parts else 0.0
            middle, left, right = (jnp.where(outside, value, each) for each in (middle, left, right))
            beyond[part, level, lead - width : lead, :] = left
            beyond[part, level, lead:tail, :] = middle
            beyond[part, level, tail : tail + width, :] = right
        place += 2 * width
    shared(rows, planes, slopes, marks)

    def before(part, k):
        if DEEP <= k < DEEP + levels:
            return own.at[part, k - DEEP]
        return beyond.at[part, k if k < DEEP else k - levels]

    def between(part, k):
        if part == parts:
            return before(part, k)
        if DEEP + 2 <= k < DEEP + levels - 2:
            return fresh.at[part, k - DEEP - 2]
        return later.at[part, k]

    def is_inner(k):
        return DEEP + 1 <= k < DEEP + levels - 1

    def stress_one(which, k):
        return stress_in.at[which, k - DEEP - 1] if is_inner(k) else stress.at[which, k]

    def extra_one(which, k):
        return extra_in.at[which, k - DEEP - 1] if is_inner(k) else extra.at[which, k]

    def stress_two(which, k):
        return stress.at[which, k]

    def extra_two(which, k):
        return extra.at[which, k]

    for k in range(1, deep - 1):
        if not is_inner(k):
            strain(rows, before, k, stress_one, extra_one)
    for k in range(2, deep - 2):
        if DEEP + 2 <= k < DEEP + levels - 2:
            continue
        ice = marks.at[0 if k < DEEP else 1 if k < DEEP + levels else 2]
        drag = marks.at[3] if k == DEEP else None
        for part, value in enumerate(moved_on(rows, before, stress_one, extra_one, k, slopes, ice, drag)):
            later[part, k, win, :] = value
    for k in range(3, deep - 3):
        strain(rows, between, k, stress_two, extra_two)
    cut = slice(WINDOW, WINDOW + columns)
    sum_u = sum_v = jnp.zeros((rows, lanes), jnp.float32)
    for k in range(DEEP, DEEP + levels):
        drag = marks.at[3] if k == DEEP else None
        values = moved_on(rows, between, stress_two, extra_two, k, slopes, marks.at[1], drag)
        for part, value in enumerate(values):
            out[part, k - DEEP] = value[cut, :]
        sum_u, sum_v = sum_u + values[0], sum_v + values[1]

    half = 0.5 / (levels * lax.axis_size("gz"))
    height = planes[1, win, :]
    slopes[0] = height * sum_u
    flux_y = along_y(height * sum_v)
    flux_x = slopes[0, WINDOW + 1 : WINDOW + columns + 1, :] - slopes[0, WINDOW - 1 : WINDOW + columns - 1, :]
    spread = half * (flux_x + flux_y[cut, :])
    first = even("gz")
    both = weight[...] + jnp.where(first, face_above[faces:, :], face_below[faces:, :])
    part_of_both = jnp.where(first, both[: columns // 2, :], both[columns // 2 :, :])
    for target in range(message.shape[0]):
        message[target, :columns, :] = spread
        message[target, columns:, :] = part_of_both


def finish(message, density, thickness, smb, face_above, moved, far_moved, far_grown, far_burden, grown, burden, sent):
    copies = [
        pltpu.make_async_copy(a, b, sent.at[i])
        for i, (a, b) in enumerate(((moved, far_moved), (grown, far_grown), (burden, far_burden)))
    ]
    copies[0].start()
    devices = message.shape[0]
    levels, columns, _ = density.shape
    count = face_above.shape[0] - columns
    place = lax.axis_index("gz")
    spread = message[0, :columns, :]
    for device in range(1, devices):
        spread = spread + message[device, :columns, :]
    over = jnp.where(even("gz"), face_above[count:, :], 0.0)
    for device in range(2, devices, 2):
        both = jnp.concatenate([message[device, columns:, :], message[device + 1, columns:, :]], axis=0)
        over = over + jnp.where(place < device, both, 0.0)
    new = thickness[...] + 0.5 * (smb[...] - spread)
    grown[...] = new
    copies[1].start()
    scaled = new * (1.0 / (levels * devices))
    for level in range(levels - 1, -1, -1):
        here = density[level]
        burden[level] = scaled * (over + 0.5 * here)
        over = over + here
    copies[2].start()
    for copy in copies:
        copy.wait()


def pairs_of(axis):
    near = [(i, i ^ 1) for i in range(lax.axis_size(axis))]
    return near, [(i + 1, j + 1) for i, j in near[:-2]]


def body(flow, fluid, density, thickness, bed, smb, mask):
    parts, levels, columns, lanes = flow.shape
    rows = columns + 2 * WINDOW
    deep = levels + 2 * DEEP
    tall = rows + 2 * MARGIN
    near_x, next_x = pairs_of("gx")
    count = lax.axis_size("gz")
    up = [(i, (i + 1) % count) for i in range(count)]
    down = [(j, i) for i, j in up]

    *_, (_, _, width, place) = side_planes(parts, levels)
    side = f32(place + width, lanes)
    faces = (parts + 1) * DEEP - 2
    corners = sum(2 * width for _, _, width in face_planes(parts))
    wide = f32(parts + 1, levels, tall, lanes)
    flat = f32(3, tall, lanes)
    plane = f32(columns, lanes)
    inputs = (flow, fluid, bed, thickness, mask, density)
    to_near, to_next, *inputs = call(
        prepare,
        (side, side, *(jax.ShapeDtypeStruct(each.shape, each.dtype) for each in inputs)),
        in_specs=[pl.BlockSpec(memory_space=pltpu.HBM)] * len(inputs),
        scratch=[pltpu.SemaphoreType.DMA((len(inputs),))],
    )(*(pltpu.with_memory_space_constraint(each, pltpu.HBM) for each in inputs))
    face = f32((faces + 1) * columns, lanes)
    to_below, to_above, state, planes, weight = call(lay, (face, face, wide, flat, plane))(*inputs)
    next_ = lax.ppermute(to_next, "gx", next_x)
    near = lax.ppermute(to_near, "gx", near_x)
    face_below = lax.ppermute(to_above, "gz", up)
    face_above = lax.ppermute(to_below, "gz", down)

    edge = f32(corners, lanes)
    state, planes, to_below, to_above = call(widen, (wide, flat, edge, edge))(state, planes, next_, near)
    edge_below = lax.ppermute(to_above, "gz", up)
    edge_above = lax.ppermute(to_below, "gz", down)

    stress, extra, fresh = call(
        inner,
        (f32(6, levels - 2, tall, lanes), f32(2, levels - 2, rows, lanes), f32(parts, levels - 4, tall, lanes)),
        scratch=[pltpu.VMEM((2, rows, lanes), jnp.float32), pltpu.VMEM((4, rows, lanes), jnp.float32)],
        cost_estimate=pl.CostEstimate(flops=INNER_COST, bytes_accessed=INNER_COST, transcendentals=0),
    )(state, planes)

    message = f32(lax.axis_size("gz"), columns + columns // 2, lanes)
    moved, message = call(
        evolve,
        (f32(*flow.shape), message),
        scratch=[
            pltpu.VMEM((parts + 1, 2 * DEEP, tall, lanes), jnp.float32),
            pltpu.VMEM((parts, deep, tall, lanes), jnp.float32),
            pltpu.VMEM((6, deep, tall, lanes), jnp.float32),
            pltpu.VMEM((2, deep, rows, lanes), jnp.float32),
            pltpu.VMEM((2, rows, lanes), jnp.float32),
            pltpu.VMEM((4, rows, lanes), jnp.float32),
        ],
    )(state, planes, weight, stress, extra, fresh, edge_below, edge_above, face_above, face_below)
    message = lax.all_to_all(message, "gz", split_axis=0, concat_axis=0, tiled=True)
    deep_plane = f32(*density.shape)
    moved, grown, burden = call(
        finish,
        (f32(*flow.shape), plane, deep_plane),
        out_specs=[pl.BlockSpec(memory_space=pltpu.HBM)] * 3,
        scratch=[
            pltpu.VMEM(plane.shape, jnp.float32),
            pltpu.VMEM(deep_plane.shape, jnp.float32),
            pltpu.SemaphoreType.DMA((3,)),
        ],
    )(message, density, thickness, smb, face_above, moved)
    return moved, grown, burden


def solution(mesh):
    level_split = P("gz", "gx", None)
    flat = P("gx", None)
    return jax.shard_map(
        body,
        mesh=mesh,
        in_specs=(P(None, "gz", "gx", None), level_split, level_split, flat, flat, flat, flat),
        out_specs=(P(None, "gz", "gx", None), flat, level_split),
        check_vma=False,
    )
```
